256 devices in a mesh: pb: 16 (over z, core), ka: 16 (over y, x).
Axes of the slice: x: 4, y: 4, z: 8, core: 2. Of those that a mesh axis runs over, the one named last changes fastest.
Arguments:
- query: bfloat16 [32768, 2048], P(('pb', 'ka')), may hold values from -6 to 6
- keys: bfloat16 [32768, 2048], P(('pb', 'ka')), may hold values from -6 to 6
- values: bfloat16 [32768, 2048], P(('pb', 'ka')), may hold values from -6 to 6
- output: bfloat16 [32768, 2048], P(('pb', 'ka')), may hold values from -6 to 6
- grad_out: bfloat16 [32768, 2048], P(('pb', 'ka')), may hold values from -48 to 48
- log_sum_exp: bfloat16 [32768, 16], P(('pb', 'ka')), may hold values from 6.5 to 7.5
- random_blocks: int32 [512, 3], P('pb'), may hold values from 0 to 511, as said below
- global_blocks: int32 [2], replicated, may hold values from 0 to 511
Outputs:
- grad_query: bfloat16 [32768, 2048], P(('pb', 'ka'))
- grad_keys: bfloat16 [32768, 2048], P(('pb', 'ka'))
- grad_values: bfloat16 [32768, 2048], P(('pb', 'ka'))
The draws below stay inside these ranges and needn't reach their ends.
Inputs may be any that keep to these rules, and one draw needn't show every extreme that they name: `random_blocks`: the random blocks of a query block lie in its segment: the 32 blocks of the 16 devices of ka that share its index of pb. Among the 6 random blocks of one device's query blocks, at most 1 lie on one device's 2 blocks, and exactly 1 on some.
All inputs are finite; a program needn't handle non-finite values.
Results may differ from the reference program's by a relative error of at most 0.0057.
Values may be sent and summed in bfloat16 or wider, within the bound.
A program may use at most 192 MiB of HBM per device.

```python
import jax
import jax.numpy as jnp
from jax import lax

HEADS = 16
HEAD_DIM = 128
BLOCK = 64
WIN_MAX = 1
RANDOM = 3
GLOBAL = 2
TOK_DEV = 128
WIDTH = 2048
QBLK = 2
CAP = 1
TOKENS = 32768
NBLK = 512
N_PB = 16
N_KA = 16


def draw_random_blocks(key, part):
    key = jax.random.fold_in(key, 11)
    devices = N_PB * N_KA
    ref_count = QBLK * RANDOM
    subkeys = jax.random.split(key, devices + 1)
    orders = jax.vmap(lambda subkey: jax.random.permutation(subkey, N_KA * CAP))(subkeys[:devices])
    peer_ids = orders[:, :ref_count] // CAP
    inside = jax.random.randint(subkeys[devices], (devices, ref_count), 0, QBLK)
    group = jnp.arange(devices, dtype=jnp.int32) // N_KA
    block_ids = (group[:, None] * N_KA + peer_ids) * QBLK + inside
    return block_ids.reshape(NBLK, RANDOM).astype(jnp.int32)


def level_of(own_key, extent, shards, smallest, high):
    loudness, own = 1.0, jax.random.fold_in(own_key, 6)
    for position, shards_of in shards:
        heights = jnp.exp(jax.random.uniform(jax.random.fold_in(own, position), (shards_of,), jnp.float32, smallest / len(shards), high / len(shards)))
        loudness = loudness * jnp.repeat(heights, extent[position] // shards_of).reshape([-1 if axis == position else 1 for axis in range(len(extent))])
    return loudness


def centred(key, extent, scale, limit, cuts=(), kind=jnp.bfloat16):
    array = jax.random.normal(key, extent, jnp.float32) * scale
    if len(cuts) > 0:
        array = level_of(key, extent, cuts, -0.22, 0.18) * array
    return jnp.clip(array, min=-limit, max=limit).astype(kind)


def setup_inputs(seed: int = 0) -> dict:
    splits = jax.random.split(jax.random.key(seed), 9)
    return {
        "query": centred(splits[0], (TOKENS, WIDTH), 1.0, 6.0, ((0, 256),)),
        "keys": centred(splits[1], (TOKENS, WIDTH), 1.0, 6.0, ((0, 256),)),
        "values": centred(splits[2], (TOKENS, WIDTH), 1.0, 6.0, ((0, 256),)),
        "output": centred(splits[3], (TOKENS, WIDTH), 1.0, 6.0, ((0, 256),)),
        "grad_out": centred(splits[4], (TOKENS, WIDTH), 8.0, 48.0, ((0, 256),)),
        "log_sum_exp": jnp.clip(6.5 + 1.0 * jax.random.uniform(splits[5], (TOKENS, HEADS), jnp.float32) ** level_of(splits[5], (TOKENS, HEADS), ((0, 256),), -0.2, 0.2), 6.5, 7.5).astype(jnp.bfloat16),
        "random_blocks": draw_random_blocks(jax.random.fold_in(splits[8], 71), 0),
        "global_blocks": jax.random.randint(splits[7], (GLOBAL,), 0, NBLK).astype(jnp.int32),
    }


def score_grads(query_rows, grad_rows, lse_rows, delta_rows, key_heads, value_heads, active):
    factor = HEAD_DIM ** -0.5
    scores = jnp.einsum("qhd,khd->hqk", query_rows.astype(jnp.float32), key_heads.astype(jnp.float32)) * factor
    shifted = scores - jnp.transpose(lse_rows.astype(jnp.float32))[:, :, None]
    weights = jnp.where(active[:, None, :], jnp.exp(shifted), jnp.float32(0.0))
    dweight = jnp.einsum("qhd,khd->hqk", grad_rows.astype(jnp.float32), value_heads.astype(jnp.float32))
    dscore = weights * (dweight - jnp.transpose(delta_rows.astype(jnp.float32))[:, :, None])
    return weights.astype(jnp.bfloat16), dscore.astype(jnp.bfloat16)


def reference(query, keys, values, output, grad_out, log_sum_exp, random_blocks, global_blocks):
    factor = HEAD_DIM ** -0.5
    feature = HEADS * HEAD_DIM
    devices = N_PB * N_KA
    rim_rows = WIN_MAX * BLOCK
    win_rows = (2 * WIN_MAX + 1) * BLOCK
    rand_rows = RANDOM * BLOCK
    glob_rows = GLOBAL * BLOCK
    ext_rows = TOK_DEV + 2 * rim_rows
    product = grad_out.astype(jnp.float32) * output.astype(jnp.float32)
    row_delta = jnp.sum(product.reshape(TOKENS, HEADS, HEAD_DIM), axis=2).astype(jnp.bfloat16)
    key_value = jnp.stack([keys, values])
    padded = jnp.pad(key_value, ((0, 0), (rim_rows, rim_rows), (0, 0)))
    kv_blocks = key_value.reshape(2, NBLK, BLOCK, feature)
    glob_flat = jnp.take(kv_blocks, global_blocks, axis=1).reshape(2, glob_rows, feature)
    offsets = jnp.arange(-WIN_MAX, WIN_MAX + 1, dtype=jnp.int32)

    def one_shard(running, device):
        totals, glob_acc = running
        base = (device * TOK_DEV).astype(jnp.int32)
        query_s = lax.dynamic_slice_in_dim(query, base, TOK_DEV, 0).reshape(QBLK, BLOCK, HEADS, HEAD_DIM)
        grad_s = lax.dynamic_slice_in_dim(grad_out, base, TOK_DEV, 0).reshape(QBLK, BLOCK, HEADS, HEAD_DIM)
        lse_s = lax.dynamic_slice_in_dim(log_sum_exp, base, TOK_DEV, 0).reshape(QBLK, BLOCK, HEADS)
        delta_s = lax.dynamic_slice_in_dim(row_delta, base, TOK_DEV, 0).reshape(QBLK, BLOCK, HEADS)
        rand_ids = lax.dynamic_slice_in_dim(random_blocks, (device * QBLK).astype(jnp.int32), QBLK, 0)
        extended = lax.dynamic_slice_in_dim(padded, base, ext_rows, 1)

        def one_block(inner_state, inputs):
            local_acc, glob_in = inner_state
            block_at, query_rows, grad_rows, lse_rows, delta_rows, block_ids = inputs
            win = lax.dynamic_slice_in_dim(extended, (block_at * BLOCK).astype(jnp.int32), win_rows, 1)
            rand_kv = jnp.take(kv_blocks, block_ids, axis=1).reshape(2, rand_rows, feature)
            key_rows = jnp.concatenate([win, rand_kv, glob_flat], 1)
            total_rows = key_rows.shape[1]
            key_heads = key_rows.reshape(2, total_rows, HEADS, HEAD_DIM)
            target = device * QBLK + block_at + offsets
            in_seq = (target >= 0) & (target < NBLK)
            near_mask = jnp.broadcast_to(in_seq[None, :], (HEADS, 2 * WIN_MAX + 1))
            active = jnp.concatenate([jnp.repeat(near_mask, BLOCK, axis=1), jnp.ones((HEADS, total_rows - win_rows), dtype=jnp.bool_)], 1)
            weights, dscore = score_grads(query_rows, grad_rows, lse_rows, delta_rows, key_heads[0], key_heads[1], active)
            value_grad = jnp.einsum("hqk,qhd->khd", weights.astype(jnp.float32), grad_rows.astype(jnp.float32))
            key_grad = jnp.einsum("hqk,qhd->khd", dscore.astype(jnp.float32), query_rows.astype(jnp.float32)) * factor
            both_grads = jnp.stack([key_grad, value_grad]).reshape(2, total_rows, feature)
            start = (block_at * BLOCK).astype(jnp.int32)
            current = lax.dynamic_slice_in_dim(local_acc, start, win_rows, 1)
            local_acc = lax.dynamic_update_slice_in_dim(local_acc, current + both_grads[:, :win_rows], start, 1)
            glob_in = glob_in + both_grads[:, total_rows - glob_rows:]
            rand_part = both_grads[:, win_rows:win_rows + rand_rows].reshape(2, RANDOM, BLOCK, feature).astype(jnp.bfloat16)
            ds_full = dscore.astype(jnp.float32)
            keys_full = key_heads[0].astype(jnp.float32)
            query_grad = jnp.einsum("hqk,khd->qhd", ds_full[:, :, :win_rows], keys_full[:win_rows]) * factor
            query_grad = query_grad + jnp.einsum("hqk,khd->qhd", ds_full[:, :, total_rows - glob_rows:], keys_full[total_rows - glob_rows:]) * factor
            rand_ds = ds_full[:, :, win_rows:win_rows + rand_rows].reshape(HEADS, BLOCK, RANDOM, BLOCK)
            rand_keys = keys_full[win_rows:win_rows + rand_rows].reshape(RANDOM, BLOCK, HEADS, HEAD_DIM)
            rand_query = (jnp.einsum("hqrk,rkhd->rqhd", rand_ds, rand_keys) * factor).astype(jnp.bfloat16)
            rand_query = lax.optimization_barrier(rand_query).astype(jnp.float32)
            query_grad = query_grad + jnp.sum(rand_query, axis=0)
            return (local_acc, glob_in), (query_grad.astype(jnp.bfloat16), rand_part)

        start_acc = jnp.zeros((2, ext_rows, feature), jnp.float32)
        xs = (jnp.arange(QBLK, dtype=jnp.int32), query_s, grad_s, lse_s, delta_s, rand_ids)
        (local_acc, glob_acc), (query_grads, rand_parts) = lax.scan(one_block, (start_acc, glob_acc), xs)
        left_rim = lax.optimization_barrier(local_acc[:, :rim_rows].astype(jnp.bfloat16)).astype(jnp.float32)
        right_rim = lax.optimization_barrier(local_acc[:, rim_rows + TOK_DEV:].astype(jnp.bfloat16)).astype(jnp.float32)
        region = jnp.concatenate([left_rim, local_acc[:, rim_rows:rim_rows + TOK_DEV], right_rim], 1)
        region = region.reshape(2, QBLK + 2 * WIN_MAX, BLOCK, feature)
        block_start = (device * QBLK).astype(jnp.int32)
        current = lax.dynamic_slice_in_dim(totals, block_start, QBLK + 2 * WIN_MAX, 1)
        totals = lax.dynamic_update_slice_in_dim(totals, current + region, block_start, 1)
        rand_flat = jnp.transpose(rand_parts, (1, 0, 2, 3, 4)).reshape(2, QBLK * RANDOM, BLOCK, feature)
        rand_flat = lax.optimization_barrier(rand_flat).astype(jnp.float32)
        totals = totals.at[:, rand_ids.reshape(-1) + WIN_MAX].add(rand_flat)
        return (totals, glob_acc), query_grads.reshape(TOK_DEV, feature)

    totals = jnp.zeros((2, NBLK + 2 * WIN_MAX, BLOCK, feature), jnp.float32)
    glob_acc = jnp.zeros((2, glob_rows, feature), jnp.float32)
    (totals, glob_acc), query_all = lax.scan(one_shard, (totals, glob_acc), jnp.arange(devices, dtype=jnp.int32))
    totals = totals.at[:, global_blocks + WIN_MAX].add(glob_acc.reshape(2, GLOBAL, BLOCK, feature))
    summed = totals[:, WIN_MAX:WIN_MAX + NBLK].reshape(2, TOKENS, feature)
    grad_query = query_all.reshape(TOKENS, feature)
    return grad_query, summed[0].astype(jnp.bfloat16), summed[1].astype(jnp.bfloat16)
```

```python
import functools

import jax
import jax.numpy as jnp
from jax import lax
from jax.experimental import pallas as pl
from jax.experimental.pallas import tpu as pltpu
from jax.sharding import PartitionSpec as P

HEADS = 16
DIM = 128
BLOCK = 64
RANDOM = 3
GLOBAL = 2
MESH = pl.DeviceIdType.MESH
F32 = jnp.float32
BF16 = jnp.bfloat16
FACTOR = DIM**-0.5


def rows(index, size):
    return pl.ds(pl.multiple_of(index * size, size), size)


def rounded(value):
    return value.astype(BF16).astype(F32)


def kernel(
    n_seg, n_dev,
    ids, glob_at, glob_coef, query, keys, values, output, grad_out, lse_in,
    dq_hbm, dk_hbm, dv_hbm,
    kv, qg, acc, prefix, dq_out, dk_out, dv_out, g_tok, o_tok, stats_out, stats_in,
    glob_x, glob_rs, glob_red, glob_y, rim_kv, rim_in,
    send_in, recv_in, local_in, send_st, recv_st, send_out, recv_out, local_out,
    send_rs, recv_rs, send_ag, recv_ag, send_rim, recv_rim, tok_sem,
):
    seg = lax.axis_index("pb")
    me = lax.axis_index("ka")
    tok = 2 * BLOCK
    n_pair = n_dev
    refs = 2 * RANDOM
    seq_rows = n_dev * tok
    n_blk = 2 * n_dev

    def peer(t):
        return lax.rem(me + t, n_dev)

    def source(t):
        return lax.rem(me + n_dev - t, n_dev)

    def seg_peer(t):
        return lax.rem(seg + t, n_seg)

    def seg_source(t):
        return lax.rem(seg + n_seg - t, n_seg)

    def each(lo, hi, body):
        def step(t, carry):
            body(t)
            return carry

        lax.fori_loop(lo, hi, step, 0)

    def columns(j):
        return pl.ds(pl.multiple_of(j * DIM, DIM), DIM)

    barrier = pltpu.get_barrier_semaphore()

    def greet(t):
        pl.semaphore_signal(barrier, inc=1, device_id=(seg, peer(t)), device_id_type=MESH)

    def greet_seg(t):
        pl.semaphore_signal(barrier, inc=1, device_id=(seg_peer(t), me), device_id_type=MESH)

    each(1, n_dev, greet)
    each(1, n_seg, greet_seg)

    tok_g = pltpu.make_async_copy(grad_out, g_tok, tok_sem.at[0])
    tok_o = pltpu.make_async_copy(output, o_tok, tok_sem.at[1])
    tok_g.start()
    tok_o.start()

    inputs = (keys, values, query, grad_out)

    def landing(a, j):
        half = pl.ds((a % 2) * DIM, DIM)
        if a < 2:
            return kv.at[pl.ds(1 + 2 * j, 2), :, half]
        return qg.at[pl.ds(2 * j, 2), :, half]

    def head_in(a, j):
        return pltpu.make_async_remote_copy(
            src_ref=inputs[a].at[:, :, columns(j)],
            dst_ref=landing(a, me),
            send_sem=send_in.at[a, j],
            recv_sem=recv_in.at[a, me],
            device_id=(seg, j),
            device_id_type=MESH,
        )

    def head_in_from(a, j):
        return pltpu.make_async_remote_copy(
            src_ref=inputs[a].at[:, :, columns(j)],
            dst_ref=landing(a, j),
            send_sem=send_in.at[a, j],
            recv_sem=recv_in.at[a, j],
            device_id=(seg, j),
            device_id_type=MESH,
        )

    def own_in(a):
        return pltpu.make_async_copy(
            inputs[a].at[:, :, columns(me)], landing(a, me), local_in.at[a]
        )

    for a in range(4):
        own_in(a).start()

    pl.semaphore_wait(barrier, n_dev + n_seg - 2)

    def send_kv(t):
        head_in(0, peer(t)).start()
        head_in(1, peer(t)).start()

    def send_qg(t):
        head_in(2, peer(t)).start()
        head_in(3, peer(t)).start()

    each(1, n_dev, send_kv)
    each(1, n_dev, send_qg)

    lse_t = jnp.transpose(lse_in[...].astype(F32))
    tok_g.wait()
    tok_o.wait()
    lane = lax.broadcasted_iota(jnp.int32, (tok, HEADS), 1)
    delta = jnp.zeros((tok, HEADS), F32)
    for j in range(HEADS):
        part = pl.ds(j * DIM, DIM)
        product = g_tok[:, :, part].astype(F32) * o_tok[:, :, part].astype(F32)
        product = product.reshape(tok, DIM)
        delta = jnp.where(lane == j, jnp.sum(product, axis=1, keepdims=True), delta)
    delta_t = jnp.transpose(delta.astype(BF16).astype(F32))
    for j in range(HEADS):
        stats_out[j, 0:1, :] = lse_t[j : j + 1, :]
        stats_out[j, 1:2, :] = delta_t[j : j + 1, :]

    def stat(j, slot):
        return pltpu.make_async_remote_copy(
            src_ref=stats_out.at[j],
            dst_ref=stats_in.at[slot],
            send_sem=send_st.at[j],
            recv_sem=recv_st.at[slot],
            device_id=(seg, j),
            device_id_type=MESH,
        )

    each(1, n_dev, lambda t: stat(peer(t), me).start())
    stats_in[me] = stats_out[me]

    acc[...] = jnp.zeros_like(acc)
    prefix[0] = jnp.zeros_like(prefix[0])
    rim_zero = jnp.zeros((BLOCK, 2 * DIM), BF16)

    @pl.when(seg == 0)
    def _():
        kv[0] = rim_zero

    @pl.when(seg == n_seg - 1)
    def _():
        kv[n_blk + 1] = rim_zero

    own_in(0).wait()
    own_in(1).wait()

    def wait_kv(t):
        head_in_from(0, source(t)).wait_recv()
        head_in_from(1, source(t)).wait_recv()

    each(1, n_dev, wait_kv)

    def rim_copy(side, src, dst, u, target):
        return pltpu.make_async_remote_copy(
            src_ref=src,
            dst_ref=dst,
            send_sem=send_rim.at[u, side],
            recv_sem=recv_rim.at[u, side],
            device_id=(target, me),
            device_id_type=MESH,
        )

    kv_up = rim_copy(
        0, kv.at[n_blk], rim_kv.at[0], 0, seg_peer(1)
    )
    kv_down = rim_copy(
        1, kv.at[1], rim_kv.at[1], 0, seg_source(1)
    )
    grad_up = rim_copy(
        0, acc.at[pl.ds(BLOCK + seq_rows, BLOCK)], rim_in.at[0], 1, seg_peer(1)
    )
    grad_down = rim_copy(1, acc.at[pl.ds(0, BLOCK)], rim_in.at[1], 1, seg_source(1))
    has_next = seg < n_seg - 1
    has_prev = seg > 0

    @pl.when(has_next)
    def _():
        kv_up.start()

    @pl.when(has_prev)
    def _():
        kv_down.start()

    def scatter(u, c):
        return pltpu.make_async_remote_copy(
            src_ref=glob_x.at[u, rows(c, 8)],
            dst_ref=glob_rs.at[u, seg],
            send_sem=send_rs.at[u, c],
            recv_sem=recv_rs.at[u, seg],
            device_id=(c, me),
            device_id_type=MESH,
        )

    def scatter_from(u, c):
        return pltpu.make_async_remote_copy(
            src_ref=glob_x.at[u, rows(c, 8)],
            dst_ref=glob_rs.at[u, c],
            send_sem=send_rs.at[u, c],
            recv_sem=recv_rs.at[u, c],
            device_id=(c, me),
            device_id_type=MESH,
        )

    def spread(u, c):
        return pltpu.make_async_remote_copy(
            src_ref=glob_red.at[u],
            dst_ref=glob_y.at[u, rows(seg, 8)],
            send_sem=send_ag.at[u, c],
            recv_sem=recv_ag.at[u, seg],
            device_id=(c, me),
            device_id_type=MESH,
        )

    def spread_from(u, c):
        return pltpu.make_async_remote_copy(
            src_ref=glob_red.at[u],
            dst_ref=glob_y.at[u, rows(c, 8)],
            send_sem=send_ag.at[u, c],
            recv_sem=recv_ag.at[u, c],
            device_id=(c, me),
            device_id_type=MESH,
        )

    def sum_start(u):
        each(1, n_seg, lambda t: scatter(u, seg_peer(t)).start())

    def sum_middle(u):
        each(1, n_seg, lambda t: scatter_from(u, seg_source(t)).wait_recv())
        total = lax.fori_loop(
            1,
            n_seg,
            lambda t, total: total + glob_rs[u, seg_source(t)],
            glob_x[u, rows(seg, 8), :],
        )
        glob_red[u] = total
        glob_y[u, rows(seg, 8), :] = total
        each(1, n_seg, lambda t: spread(u, seg_peer(t)).start())

    def sum_end(u):
        each(1, n_seg, lambda t: spread_from(u, seg_source(t)).wait_recv())

    def sum_drain(u):
        def one(t):
            scatter(u, seg_peer(t)).wait_send()
            spread(u, seg_peer(t)).wait_send()

        each(1, n_seg, one)

    def key_block(at):
        return kv[at + 1]

    for i in range(GLOBAL):
        glob_x[0, pl.ds(i * BLOCK, BLOCK), :] = (
            key_block(glob_at[i]).astype(F32) * glob_coef[n_blk * GLOBAL + i]
        )
    sum_start(0)
    sum_middle(0)

    @pl.when(has_prev)
    def _():
        kv_up.wait_recv()
        kv[0] = rim_kv[0]

    @pl.when(has_next)
    def _():
        kv_down.wait_recv()
        kv[n_blk + 1] = rim_kv[1]

    sum_end(0)
    glob_x[1] = jnp.zeros((GLOBAL * BLOCK, 2 * DIM), F32)

    def out_copy(a, j):
        out, held = ((dq_hbm, dq_out), (dk_hbm, dk_out), (dv_hbm, dv_out))[a]
        return pltpu.make_async_remote_copy(
            src_ref=held.at[rows(j, tok)],
            dst_ref=out.at[:, columns(me)],
            send_sem=send_out.at[a, j],
            recv_sem=recv_out.at[a, me],
            device_id=(seg, j),
            device_id_type=MESH,
        )

    def out_from(a, j):
        out, held = ((dq_hbm, dq_out), (dk_hbm, dk_out), (dv_hbm, dv_out))[a]
        return pltpu.make_async_remote_copy(
            src_ref=held.at[rows(j, tok)],
            dst_ref=out.at[:, columns(j)],
            send_sem=send_out.at[a, j],
            recv_sem=recv_out.at[a, j],
            device_id=(seg, j),
            device_id_type=MESH,
        )

    def own_out(a):
        out, held = ((dq_hbm, dq_out), (dk_hbm, dk_out), (dv_hbm, dv_out))[a]
        return pltpu.make_async_copy(
            held.at[rows(me, tok)], out.at[:, columns(me)], local_out.at[a]
        )

    def one_pair(t):
        d = source(t)

        @pl.when(t == 0)
        def _():
            own_in(2).wait()
            own_in(3).wait()

        @pl.when(t > 0)
        def _():
            head_in_from(2, d).wait_recv()
            head_in_from(3, d).wait_recv()
            stat(d, d).wait_recv()

        both = qg[pl.ds(2 * d, 2)].reshape(tok, 2 * DIM)
        q = both[:, :DIM]
        g = both[:, DIM:]
        lse = stats_in[d, 0:1, :]
        row_delta = stats_in[d, 1:2, :]
        zero = jnp.zeros((tok, DIM), BF16)
        into = jnp.concatenate(
            [jnp.concatenate([q, zero], 1), jnp.concatenate([zero, g], 1)], 0
        )
        back = jnp.concatenate(
            [jnp.concatenate([g, zero], 1), jnp.concatenate([zero, q], 1)], 0
        )

        def entries(block, active):
            both = lax.dot_general(
                block, into, (((1,), (1,)), ((), ())), preferred_element_type=F32
            )
            weights = jnp.exp(both[:, :DIM] * FACTOR - lse)
            if active is not None:
                weights = jnp.where(active, weights, 0.0)
            dscore = (weights * (both[:, DIM:] - row_delta)).astype(BF16)
            grads = jnp.dot(
                jnp.concatenate([weights.astype(BF16), dscore], 1),
                back,
                preferred_element_type=F32,
            )
            part = lax.dot_general(
                dscore, block[:, :DIM], (((0,), (0,)), ((), ())), preferred_element_type=F32
            )
            return grads, part

        lane = lax.broadcasted_iota(jnp.int32, (1, 2 * DIM), 1)
        scale = jnp.where(lane < DIM, 1.0, FACTOR).astype(F32)

        def places(count):
            key_at = lax.broadcasted_iota(jnp.int32, (count, tok), 0)
            query_at = lax.broadcasted_iota(jnp.int32, (count, tok), 1) // BLOCK
            return key_at, query_at

        key_at, query_at = places(4 * BLOCK)
        key_at = key_at // BLOCK
        absolute = seg * n_blk + 2 * d - 1 + key_at
        active = (
            (key_at >= query_at)
            & (key_at <= query_at + 2)
            & (absolute >= 0)
            & (absolute < n_seg * n_blk)
        )
        window = kv[pl.ds(2 * d, 4)].reshape(4 * BLOCK, 2 * DIM)
        grads, dq = entries(window, active)
        grads = grads * scale
        above = pl.ds(pl.multiple_of(d * tok, tok), BLOCK)
        inside = pl.ds(pl.multiple_of(d * tok + BLOCK, BLOCK), tok)
        below = pl.ds(pl.multiple_of(d * tok + BLOCK + tok, BLOCK), BLOCK)
        acc[above, :] += rounded(grads[:BLOCK])
        acc[inside, :] += grads[BLOCK : BLOCK + tok]
        acc[below, :] += rounded(grads[BLOCK + tok :])

        grads, part = entries(glob_y[0].astype(BF16), None)
        glob_x[1] += grads * scale
        dq = (dq + part) * FACTOR

        key_at, query_at = places(2 * BLOCK)
        active = key_at // BLOCK == query_at
        for r in range(RANDOM):
            pair_at = [t * refs + r, t * refs + RANDOM + r]
            listed = jnp.concatenate([key_block(ids[at]) for at in pair_at], 0)
            grads, part = entries(listed, active)
            grads = rounded(grads * scale)
            dq += rounded(part * FACTOR)
            for i, at in enumerate(pair_at):
                before = prefix[ids[n_pair * refs + at]]
                prefix[at + 1] = grads[i * BLOCK : (i + 1) * BLOCK] + before

        dq_out[rows(d, tok), :] = dq.astype(BF16)

        @pl.when(t == 0)
        def _():
            own_out(0).start()

        @pl.when(t > 0)
        def _():
            out_copy(0, d).start()

    each(0, n_pair, one_pair)

    @pl.when(has_next)
    def _():
        grad_up.start()

    @pl.when(has_prev)
    def _():
        grad_down.start()

    sum_start(1)
    sum_middle(1)

    @pl.when(has_prev)
    def _():
        grad_up.wait_recv()
        acc[pl.ds(BLOCK, BLOCK), :] += rim_in[0]

    @pl.when(has_next)
    def _():
        grad_down.wait_recv()
        acc[pl.ds(seq_rows, BLOCK), :] += rim_in[1]

    sum_end(1)

    def finish(t):
        d = source(t)
        for i in range(2):
            b = 2 * d + i
            at = pl.ds(pl.multiple_of(b * BLOCK, BLOCK), BLOCK)
            total = acc[pl.ds(pl.multiple_of(BLOCK + b * BLOCK, BLOCK), BLOCK), :]
            total += prefix[ids[2 * n_pair * refs + b]]
            for j in range(GLOBAL):
                total += glob_y[1, pl.ds(j * BLOCK, BLOCK), :] * glob_coef[b * GLOBAL + j]
            dv_out[at, :] = total[:, :DIM].astype(BF16)
            dk_out[at, :] = total[:, DIM:].astype(BF16)

        @pl.when(t == 0)
        def _():
            own_out(1).start()
            own_out(2).start()

        @pl.when(t > 0)
        def _():
            out_copy(1, d).start()
            out_copy(2, d).start()

    each(0, n_pair, finish)

    sum_drain(0)
    sum_drain(1)

    @pl.when(has_next)
    def _():
        kv_up.wait_send()
        grad_up.wait_send()

    @pl.when(has_prev)
    def _():
        kv_down.wait_send()
        grad_down.wait_send()

    def drain(t):
        for a in range(4):
            head_in(a, peer(t)).wait_send()
        stat(peer(t), me).wait_send()
        for a in range(3):
            out_copy(a, peer(t)).wait_send()

    def drain_recv(t):
        for a in range(3):
            out_from(a, source(t)).wait_recv()

    each(1, n_dev, drain)
    for a in range(3):
        own_out(a).wait()
    each(1, n_dev, drain_recv)


def shards(query, keys, values, output, grad_out, log_sum_exp, random_blocks, global_blocks):
    tok, width = query.shape
    query, keys, values, output, grad_out = (
        x.reshape(2, BLOCK, width) for x in (query, keys, values, output, grad_out)
    )
    n_seg, n_dev = lax.axis_size("pb"), lax.axis_size("ka")
    seg, me = lax.axis_index("pb"), lax.axis_index("ka")
    refs = 2 * RANDOM
    n_blk = 2 * n_dev
    count = n_dev * refs

    upside = random_blocks.reshape(n_dev, refs)[::-1] % n_blk
    listed = lax.dynamic_slice_in_dim(
        jnp.concatenate([upside, upside], 0), n_dev - 1 - me, n_dev, 0
    ).reshape(count)
    order = jnp.arange(count, dtype=jnp.int32)
    asked = jnp.concatenate([listed, jnp.arange(n_blk, dtype=jnp.int32)])
    limit = jnp.concatenate([order, jnp.full((n_blk,), count, jnp.int32)])
    same = (asked[:, None] == listed[None, :]) & (order[None, :] < limit[:, None])
    last = jnp.max(jnp.where(same, order[None, :] + 1, 0), axis=1)
    ids = jnp.concatenate([listed, last]).astype(jnp.int32)
    glob_at = global_blocks % n_blk
    mine = global_blocks // n_blk == seg
    owned = mine[None, :] & (glob_at[None, :] == jnp.arange(n_blk)[:, None])
    glob_coef = jnp.concatenate([owned.reshape(-1), mine]).astype(F32)

    smem = pl.BlockSpec(memory_space=pltpu.SMEM)
    hbm = pl.BlockSpec(memory_space=pl.ANY)
    vmem = pl.BlockSpec(memory_space=pltpu.VMEM)
    dma = pltpu.SemaphoreType.DMA
    seq = n_dev * tok
    glob = GLOBAL * BLOCK
    out = jax.ShapeDtypeStruct((tok, width), BF16)
    return pl.pallas_call(
        functools.partial(kernel, n_seg, n_dev),
        out_shape=(out, out, out),
        in_specs=[smem, smem, smem, hbm, hbm, hbm, hbm, hbm, vmem],
        out_specs=(hbm, hbm, hbm),
        scratch_shapes=[
            pltpu.VMEM((n_blk + 2, BLOCK, 2 * DIM), BF16),
            pltpu.VMEM((n_blk, BLOCK, 2 * DIM), BF16),
            pltpu.VMEM((seq + 2 * BLOCK, 2 * DIM), F32),
            pltpu.VMEM((count + 1, BLOCK, 2 * DIM), F32),
            pltpu.VMEM((seq, DIM), BF16),
            pltpu.VMEM((seq, DIM), BF16),
            pltpu.VMEM((seq, DIM), BF16),
            pltpu.VMEM((2, BLOCK, width), BF16),
            pltpu.VMEM((2, BLOCK, width), BF16),
            pltpu.VMEM((n_dev, 8, tok), F32),
            pltpu.VMEM((n_dev, 8, tok), F32),
            pltpu.VMEM((2, glob, 2 * DIM), F32),
            pltpu.VMEM((2, n_seg, 8, 2 * DIM), F32),
            pltpu.VMEM((2, 8, 2 * DIM), F32),
            pltpu.VMEM((2, glob, 2 * DIM), F32),
            pltpu.VMEM((2, BLOCK, 2 * DIM), BF16),
            pltpu.VMEM((2, BLOCK, 2 * DIM), F32),
            dma((4, n_dev)),
            dma((4, n_dev)),
            dma((4,)),
            dma((n_dev,)),
            dma((n_dev,)),
            dma((3, n_dev)),
            dma((3, n_dev)),
            dma((3,)),
            dma((2, n_seg)),
            dma((2, n_seg)),
            dma((2, n_seg)),
            dma((2, n_seg)),
            dma((2, 2)),
            dma((2, 2)),
            dma((2,)),
        ],
        compiler_params=pltpu.CompilerParams(
            collective_id=0, has_side_effects=True, vmem_limit_bytes=48 * 2**20
        ),
        cost_estimate=pl.CostEstimate(
            flops=2**32, bytes_accessed=2**23, transcendentals=2**21
        ),
    )(ids, glob_at, glob_coef, query, keys, values, output, grad_out, log_sum_exp)


def solution(mesh):
    both = P(("pb", "ka"), None)
    return jax.shard_map(
        shards,
        mesh=mesh,
        in_specs=(both, both, both, both, both, both, P("pb", None), P()),
        out_specs=(both, both, both),
        check_vma=False,
    )
```

```python
import functools

import jax
import jax.numpy as jnp
from jax import lax
from jax.experimental import pallas as pl
from jax.experimental.pallas import tpu as pltpu
from jax.sharding import PartitionSpec as P

HEADS = 16
DIM = 128
BLOCK = 64
RANDOM = 3
GLOBAL = 2
QG_EARLY = 3
QG_MIDDLE = 7
RANDOM_EARLY = 8
MESH = pl.DeviceIdType.MESH
F32 = jnp.float32
BF16 = jnp.bfloat16
FACTOR = DIM**-0.5


def rows(index, size):
    return pl.ds(pl.multiple_of(index * size, size), size)


def rounded(value):
    return value.astype(BF16).astype(F32)


def kernel(
    n_seg, n_dev,
    listed_at, glob_id, query, keys, values, output, grad_out, lse_t,
    dq_hbm, dk_hbm, dv_hbm,
    kv, qg, acc, prefix, dq_acc, dq_out, dk_out, dv_out, g_tok, o_tok, stats_out, stats_in,
    glob_x, glob_rs, glob_red, glob_y, glob_kv, rim_kv, rim_in, table, links,
    send_in, recv_kv, recv_qg, local_in, send_st, recv_st, send_out, recv_out, local_out,
    send_rs, recv_rs, send_ag, recv_ag, send_rim, recv_rim, tok_sem, table_sem,
):
    seg = lax.axis_index("pb")
    me = lax.axis_index("ka")
    tok = 2 * BLOCK
    n_pair = n_dev
    refs = 2 * RANDOM
    seq_rows = n_dev * tok
    n_blk = 2 * n_dev

    def peer(t):
        return lax.rem(me + t, n_dev)

    def source(t):
        return lax.rem(me + n_dev - t, n_dev)

    def seg_peer(t):
        return lax.rem(seg + t, n_seg)

    def seg_source(t):
        return lax.rem(seg + n_seg - t, n_seg)

    def each(lo, hi, body):
        def step(t, carry):
            body(t)
            return carry

        lax.fori_loop(lo, hi, step, 0)

    def slot_of(phase, t, k):
        return 1 + 2 * t + k if phase == 0 else 1 + 2 * n_pair + 2 * (RANDOM - 1) * t + k

    def listed(d, e):
        return lax.rem(listed_at[e % RANDOM, 2 * d + e // RANDOM], n_blk)

    def arrived(ref, sem):
        pltpu.make_async_copy(ref, ref, sem).wait()

    def columns(j):
        return pl.ds(pl.multiple_of(j * DIM, DIM), DIM)

    barrier = pltpu.get_barrier_semaphore()

    def greet(t):
        pl.semaphore_signal(barrier, inc=1, device_id=(seg, peer(t)), device_id_type=MESH)

    def greet_seg(t):
        pl.semaphore_signal(barrier, inc=1, device_id=(seg_peer(t), me), device_id_type=MESH)

    each(1, n_dev, greet)
    each(1, n_seg, greet_seg)

    tok_g = pltpu.make_async_copy(grad_out, g_tok, tok_sem.at[0])
    tok_o = pltpu.make_async_copy(output, o_tok, tok_sem.at[1])
    tok_g.start()
    tok_o.start()

    inputs = (keys, values, query, grad_out)

    def landing(a, j):
        half = pl.ds((a % 2) * DIM, DIM)
        if a < 2:
            return kv.at[pl.ds(1 + 2 * j, 2), :, half]
        return qg.at[pl.ds(2 * j, 2), :, half]

    def head_in(a, j):
        return pltpu.make_async_remote_copy(
            src_ref=inputs[a].at[:, :, columns(j)],
            dst_ref=landing(a, me),
            send_sem=send_in.at[a // 2],
            recv_sem=recv_kv if a < 2 else recv_qg.at[me],
            device_id=(seg, j),
            device_id_type=MESH,
        )

    def own_in(a):
        return pltpu.make_async_copy(
            inputs[a].at[:, :, columns(me)], landing(a, me), local_in.at[a]
        )

    for a in range(4):
        own_in(a).start()

    pl.semaphore_wait(barrier, n_dev + n_seg - 2)

    def send_kv(t):
        head_in(0, peer(t)).start()
        head_in(1, peer(t)).start()

    def send_qg(t):
        head_in(2, peer(t)).start()
        head_in(3, peer(t)).start()

    each(1, n_dev, send_kv)

    tok_g.wait()
    tok_o.wait()
    lane = lax.broadcasted_iota(jnp.int32, (tok, HEADS), 1)
    delta = jnp.zeros((tok, HEADS), F32)
    for j in range(HEADS):
        part = pl.ds(j * DIM, DIM)
        product = g_tok[:, :, part].astype(F32) * o_tok[:, :, part].astype(F32)
        product = product.reshape(tok, DIM)
        delta = jnp.where(lane == j, jnp.sum(product, axis=1, keepdims=True), delta)
    lse_rows = lse_t[...].astype(F32)
    delta_t = jnp.transpose(delta.astype(BF16).astype(F32))
    for j in range(HEADS):
        stats_out[j, 0:1, :] = lse_rows[j : j + 1, :]
        stats_out[j, 1:2, :] = delta_t[j : j + 1, :]

    def stat(j):
        return pltpu.make_async_remote_copy(
            src_ref=stats_out.at[j],
            dst_ref=stats_in.at[me],
            send_sem=send_st,
            recv_sem=recv_st,
            device_id=(seg, j),
            device_id_type=MESH,
        )

    each(1, n_dev, lambda t: stat(peer(t)).start())
    stats_in[me] = stats_out[me]

    acc[...] = jnp.zeros_like(acc)
    prefix[0] = jnp.zeros_like(prefix[0])
    rim_zero = jnp.zeros((BLOCK, 2 * DIM), BF16)

    @pl.when(seg == 0)
    def _():
        kv[0] = rim_zero

    @pl.when(seg == n_seg - 1)
    def _():
        kv[n_blk + 1] = rim_zero

    block_lane = lax.broadcasted_iota(jnp.int32, (1, DIM), 1)

    def remember(phase, first, last):
        def step(t, latest):
            table[pl.ds(phase * n_pair + t, 1), :] = latest
            for k, e in enumerate(i * RANDOM + r for r in range(first, last) for i in range(2)):
                slot = slot_of(phase, t, k)
                latest = jnp.where(block_lane == listed(source(t), e), slot, latest)
            return latest

        return step

    latest = jnp.zeros((1, DIM), jnp.int32)
    latest = lax.fori_loop(0, n_pair, remember(0, 0, 1), latest)
    latest = lax.fori_loop(0, n_pair, remember(1, 1, RANDOM), latest)
    table[pl.ds(2 * n_pair, 1), :] = latest
    to_links = pltpu.make_async_copy(table, links, table_sem)
    to_links.start()

    each(1, QG_EARLY, send_qg)
    to_links.wait()

    own_in(0).wait()
    own_in(1).wait()

    arrived(kv.at[pl.ds(0, 2 * (n_dev - 1))], recv_kv)

    def rim_copy(side, src, dst, u, target):
        return pltpu.make_async_remote_copy(
            src_ref=src,
            dst_ref=dst,
            send_sem=send_rim.at[u, side],
            recv_sem=recv_rim.at[u, side],
            device_id=(target, me),
            device_id_type=MESH,
        )

    kv_up = rim_copy(
        0, kv.at[n_blk], rim_kv.at[0], 0, seg_peer(1)
    )
    kv_down = rim_copy(
        1, kv.at[1], rim_kv.at[1], 0, seg_source(1)
    )
    grad_up = rim_copy(
        0, acc.at[pl.ds(BLOCK + seq_rows, BLOCK)], rim_in.at[0], 1, seg_peer(1)
    )
    grad_down = rim_copy(1, acc.at[pl.ds(0, BLOCK)], rim_in.at[1], 1, seg_source(1))
    has_next = seg < n_seg - 1
    has_prev = seg > 0

    @pl.when(has_next)
    def _():
        kv_up.start()

    @pl.when(has_prev)
    def _():
        kv_down.start()

    def scatter(u, c):
        return pltpu.make_async_remote_copy(
            src_ref=glob_x.at[u, rows(c, 8)],
            dst_ref=glob_rs.at[u, seg],
            send_sem=send_rs.at[u],
            recv_sem=recv_rs.at[u],
            device_id=(c, me),
            device_id_type=MESH,
        )

    def spread(u, c):
        return pltpu.make_async_remote_copy(
            src_ref=glob_red.at[u],
            dst_ref=glob_y.at[u, rows(seg, 8)],
            send_sem=send_ag.at[u],
            recv_sem=recv_ag.at[u],
            device_id=(c, me),
            device_id_type=MESH,
        )

    others = pl.ds(0, n_seg - 1)
    others_rows = pl.ds(0, 8 * (n_seg - 1))

    def sum_start(u):
        each(1, n_seg, lambda t: scatter(u, seg_peer(t)).start())

    def sum_middle(u):
        arrived(glob_rs.at[u, others], recv_rs.at[u])
        total = glob_x[u, rows(seg, 8), :]
        for t in range(1, n_seg):
            total += glob_rs[u, seg_source(t)]
        glob_red[u] = total
        glob_y[u, rows(seg, 8), :] = total
        each(1, n_seg, lambda t: spread(u, seg_peer(t)).start())

    def sum_end(u):
        arrived(glob_y.at[u, others_rows], recv_ag.at[u])

    def sum_drain(u):
        arrived(glob_rs.at[u, others], send_rs.at[u])
        arrived(glob_y.at[u, others_rows], send_ag.at[u])

    def key_block(at):
        return kv[at + 1]

    def owned(i):
        return jnp.where(glob_id[i] // n_blk == seg, 1.0, 0.0).astype(F32)

    for i in range(GLOBAL):
        glob_x[0, pl.ds(i * BLOCK, BLOCK), :] = (
            key_block(lax.rem(glob_id[i], n_blk)).astype(F32) * owned(i)
        )
    sum_start(0)
    each(QG_EARLY, QG_MIDDLE, send_qg)
    glob_x[1] = jnp.zeros((GLOBAL * BLOCK, 2 * DIM), F32)

    def out_copy(a, j):
        out, held = ((dq_hbm, dq_out), (dk_hbm, dk_out), (dv_hbm, dv_out))[a]
        return pltpu.make_async_remote_copy(
            src_ref=held.at[rows(j, tok)],
            dst_ref=out.at[:, columns(me)],
            send_sem=send_out.at[a],
            recv_sem=recv_out.at[a],
            device_id=(seg, j),
            device_id_type=MESH,
        )

    def own_out(a):
        out, held = ((dq_hbm, dq_out), (dk_hbm, dk_out), (dv_hbm, dv_out))[a]
        return pltpu.make_async_copy(
            held.at[rows(me, tok)], out.at[:, columns(me)], local_out.at[a]
        )

    lane = lax.broadcasted_iota(jnp.int32, (1, 2 * DIM), 1)
    scale = jnp.where(lane < DIM, 1.0, FACTOR).astype(F32)

    def pair(d):
        both = qg[pl.ds(2 * d, 2)].reshape(tok, 2 * DIM)
        q = both[:, :DIM]
        g = both[:, DIM:]
        lse = stats_in[d, 0:1, :]
        row_delta = stats_in[d, 1:2, :]
        zero = jnp.zeros((tok, DIM), BF16)
        into = jnp.concatenate(
            [jnp.concatenate([q, zero], 1), jnp.concatenate([zero, g], 1)], 0
        )
        back = jnp.concatenate(
            [jnp.concatenate([g, zero], 1), jnp.concatenate([zero, q], 1)], 0
        )

        def entries(block, active):
            both = lax.dot_general(
                block, into, (((1,), (1,)), ((), ())), preferred_element_type=F32
            )
            weights = jnp.exp(both[:, :DIM] * FACTOR - lse)
            if active is not None:
                weights = jnp.where(active, weights, 0.0)
            dscore = (weights * (both[:, DIM:] - row_delta)).astype(BF16)
            grads = jnp.dot(
                jnp.concatenate([weights.astype(BF16), dscore], 1),
                back,
                preferred_element_type=F32,
            )
            return grads * scale, dscore

        return entries

    def query_grad(dscore, block):
        return FACTOR * lax.dot_general(
            dscore, block[:, :DIM], (((0,), (0,)), ((), ())), preferred_element_type=F32
        )

    def random_grads(grads, phase, t, found):
        grads = rounded(grads)
        for k, b in enumerate(found):
            before = prefix[links[phase * n_pair + t, b]]
            prefix[slot_of(phase, t, k)] = grads[k * BLOCK : (k + 1) * BLOCK] + before

    def places(count):
        key_at = lax.broadcasted_iota(jnp.int32, (count, tok), 0)
        query_at = lax.broadcasted_iota(jnp.int32, (count, tok), 1) // BLOCK
        return key_at // BLOCK, query_at

    def first_part(t):
        d = source(t)

        @pl.when(t == 0)
        def _():
            own_in(2).wait()
            own_in(3).wait()

        @pl.when(t > 0)
        def _():
            arrived(qg.at[pl.ds(2 * d, 2)], recv_qg.at[d])

        @pl.when((d == 0) & has_prev)
        def _():
            kv_up.wait_recv()
            kv[0] = rim_kv[0]

        @pl.when((d == n_pair - 1) & has_next)
        def _():
            kv_down.wait_recv()
            kv[n_blk + 1] = rim_kv[1]

        win, glob, rand = 4 * BLOCK, GLOBAL * BLOCK, 2 * BLOCK
        key_at, query_at = places(win)
        absolute = seg * n_blk + 2 * d - 1 + key_at
        near = (
            (key_at >= query_at)
            & (key_at <= query_at + 2)
            & (absolute >= 0)
            & (absolute < n_seg * n_blk)
        )
        key_at, query_at = places(rand)
        own = key_at == query_at
        whole = jnp.ones((glob, tok), jnp.bool_)
        found = [listed(d, 0), listed(d, RANDOM)]
        block = jnp.concatenate(
            [kv[pl.ds(2 * d, 4)].reshape(win, 2 * DIM), glob_kv[...]]
            + [key_block(b) for b in found],
            0,
        )
        grads, dscore = pair(d)(block, jnp.concatenate([near, whole, own], 0))
        above = pl.ds(pl.multiple_of(d * tok, tok), BLOCK)
        inside = pl.ds(pl.multiple_of(d * tok + BLOCK, BLOCK), tok)
        below = pl.ds(pl.multiple_of(d * tok + BLOCK + tok, BLOCK), BLOCK)
        acc[above, :] += rounded(grads[:BLOCK])
        acc[inside, :] += grads[BLOCK : BLOCK + tok]
        acc[below, :] += rounded(grads[BLOCK + tok : win])
        glob_x[1] += grads[win : win + glob]
        random_grads(grads[win + glob :], 0, t, found)
        dq = query_grad(dscore[: win + glob], block[: win + glob])
        dq_acc[rows(d, tok), :] = dq + rounded(query_grad(dscore[win + glob :], block[win + glob :]))

    def second_part(t):
        d = source(t)
        rand = 2 * BLOCK
        key_at, query_at = places(rand)
        own = key_at == query_at
        found = [listed(d, i * RANDOM + r) for i in range(2) for r in range(1, RANDOM)]
        by_r = [found[i * (RANDOM - 1) + r] for r in range(RANDOM - 1) for i in range(2)]
        block = jnp.concatenate([key_block(b) for b in by_r], 0)
        grads, dscore = pair(d)(block, jnp.concatenate([own] * (RANDOM - 1), 0))
        dq = dq_acc[rows(d, tok), :]
        for r in range(RANDOM - 1):
            part = slice(r * rand, (r + 1) * rand)
            dq += rounded(query_grad(dscore[part], block[part]))
        random_grads(grads, 1, t, by_r)
        dq_out[rows(d, tok), :] = dq.astype(BF16)

        @pl.when(t == 0)
        def _():
            own_out(0).start()

        @pl.when(t > 0)
        def _():
            out_copy(0, d).start()

    sum_middle(0)
    each(QG_MIDDLE, n_dev, send_qg)
    arrived(stats_in.at[pl.ds(0, n_dev - 1)], recv_st)
    sum_end(0)
    glob_kv[...] = glob_y[0].astype(BF16)
    each(0, n_pair, first_part)

    @pl.when(has_next)
    def _():
        grad_up.start()

    @pl.when(has_prev)
    def _():
        grad_down.start()

    sum_start(1)
    each(0, RANDOM_EARLY, second_part)
    sum_middle(1)
    each(RANDOM_EARLY, n_pair, second_part)

    @pl.when(has_prev)
    def _():
        grad_up.wait_recv()
        acc[pl.ds(BLOCK, BLOCK), :] += rim_in[0]

    @pl.when(has_next)
    def _():
        grad_down.wait_recv()
        acc[pl.ds(seq_rows, BLOCK), :] += rim_in[1]

    sum_end(1)

    def finish(t):
        d = source(t)
        for i in range(2):
            b = 2 * d + i
            at = pl.ds(pl.multiple_of(b * BLOCK, BLOCK), BLOCK)
            total = acc[pl.ds(pl.multiple_of(BLOCK + b * BLOCK, BLOCK), BLOCK), :]
            total += prefix[links[2 * n_pair, b]]
            for j in range(GLOBAL):
                here = jnp.where(glob_id[j] == seg * n_blk + b, 1.0, 0.0).astype(F32)
                total += glob_y[1, pl.ds(j * BLOCK, BLOCK), :] * here
            dv_out[at, :] = total[:, :DIM].astype(BF16)
            dk_out[at, :] = total[:, DIM:].astype(BF16)

        @pl.when(t == 0)
        def _():
            own_out(1).start()
            own_out(2).start()

        @pl.when(t > 0)
        def _():
            out_copy(1, d).start()
            out_copy(2, d).start()

    each(0, n_pair, finish)

    sum_drain(0)
    sum_drain(1)

    @pl.when(has_next)
    def _():
        kv_up.wait_send()
        grad_up.wait_send()

    @pl.when(has_prev)
    def _():
        kv_down.wait_send()
        grad_down.wait_send()

    most = pl.ds(0, 2 * (n_dev - 1))
    arrived(kv.at[most], send_in.at[0])
    arrived(qg.at[most], send_in.at[1])
    arrived(stats_out.at[pl.ds(0, n_dev - 1)], send_st)
    for a, (out, held) in enumerate(((dq_hbm, dq_out), (dk_hbm, dk_out), (dv_hbm, dv_out))):
        arrived(held.at[pl.ds(0, (n_dev - 1) * tok)], send_out.at[a])
        own_out(a).wait()
        arrived(out.at[:, pl.ds(0, (n_dev - 1) * DIM)], recv_out.at[a])


def shards(query, keys, values, output, grad_out, log_sum_exp, random_blocks, global_blocks):
    tok, width = query.shape
    query, keys, values, output, grad_out = (
        x.reshape(2, BLOCK, width) for x in (query, keys, values, output, grad_out)
    )
    n_seg, n_dev = lax.axis_size("pb"), lax.axis_size("ka")
    refs = 2 * RANDOM
    n_blk = 2 * n_dev
    count = n_dev * refs

    smem = pl.BlockSpec(memory_space=pltpu.SMEM)
    hbm = pl.BlockSpec(memory_space=pltpu.HBM)
    vmem = pl.BlockSpec(memory_space=pltpu.VMEM)
    dma = pltpu.SemaphoreType.DMA
    seq = n_dev * tok
    glob = GLOBAL * BLOCK
    out = jax.ShapeDtypeStruct((tok, width), BF16)
    grads = pl.pallas_call(
        functools.partial(kernel, n_seg, n_dev),
        out_shape=(out, out, out),
        in_specs=[smem, smem, hbm, hbm, hbm, hbm, hbm, vmem],
        out_specs=(hbm, hbm, hbm),
        scratch_shapes=[
            pltpu.VMEM((n_blk + 2, BLOCK, 2 * DIM), BF16),
            pltpu.VMEM((n_blk, BLOCK, 2 * DIM), BF16),
            pltpu.VMEM((seq + 2 * BLOCK, 2 * DIM), F32),
            pltpu.VMEM((count + 1, BLOCK, 2 * DIM), F32),
            pltpu.VMEM((seq, DIM), F32),
            pltpu.VMEM((seq, DIM), BF16),
            pltpu.VMEM((seq, DIM), BF16),
            pltpu.VMEM((seq, DIM), BF16),
            pltpu.VMEM((2, BLOCK, width), BF16),
            pltpu.VMEM((2, BLOCK, width), BF16),
            pltpu.VMEM((n_dev, 8, tok), F32),
            pltpu.VMEM((n_dev, 8, tok), F32),
            pltpu.VMEM((2, glob, 2 * DIM), F32),
            pltpu.VMEM((2, n_seg, 8, 2 * DIM), F32),
            pltpu.VMEM((2, 8, 2 * DIM), F32),
            pltpu.VMEM((2, glob, 2 * DIM), F32),
            pltpu.VMEM((glob, 2 * DIM), BF16),
            pltpu.VMEM((2, BLOCK, 2 * DIM), BF16),
            pltpu.VMEM((2, BLOCK, 2 * DIM), F32),
            pltpu.VMEM((2 * n_dev + 8, DIM), jnp.int32),
            pltpu.SMEM((2 * n_dev + 8, DIM), jnp.int32),
            dma((2,)),
            dma(()),
            dma((n_dev,)),
            dma((4,)),
            dma(()),
            dma(()),
            dma((3,)),
            dma((3,)),
            dma((3,)),
            dma((2,)),
            dma((2,)),
            dma((2,)),
            dma((2,)),
            dma((2, 2)),
            dma((2, 2)),
            dma((2,)),
            dma(()),
        ],
        compiler_params=pltpu.CompilerParams(
            collective_id=0, has_side_effects=True, vmem_limit_bytes=52 * 2**20
        ),
        cost_estimate=pl.CostEstimate(
            flops=2**32, bytes_accessed=2**23, transcendentals=2**21
        ),
    )(jnp.transpose(random_blocks), global_blocks, query, keys, values, output, grad_out, jnp.transpose(log_sum_exp))
    return grads


def solution(mesh):
    both = P(("pb", "ka"), None)
    return jax.shard_map(
        shards,
        mesh=mesh,
        in_specs=(both, both, both, both, both, both, P("pb", None), P()),
        out_specs=(both, both, both),
        check_vma=False,
    )
```

```python
import functools

import jax
import jax.numpy as jnp
from jax import lax
from jax.experimental import pallas as pl
from jax.experimental.pallas import tpu as pltpu
from jax.sharding import PartitionSpec as P

HEADS = 16
DIM = 128
BLOCK = 64
RANDOM = 3
GLOBAL = 2
QG_EARLY = 4
QG_MIDDLE = 12
LATE = 14
MESH = pl.DeviceIdType.MESH
F32 = jnp.float32
BF16 = jnp.bfloat16
FACTOR = DIM**-0.5


def rows(index, size):
    return pl.ds(pl.multiple_of(index * size, size), size)


def rounded(value):
    return value.astype(BF16).astype(F32)


def kernel(
    n_seg, n_dev,
    listed_at, glob_id, query, keys, values, output, grad_out, lse_t,
    dq_hbm, dk_hbm, dv_hbm,
    kv, qg, acc, prefix, dq_acc, dq_out, dk_out, dv_out, g_tok, o_tok, stats_out, stats_in,
    glob_x, glob_rs, glob_red, glob_y, glob_kv, rim_kv, rim_in, table, links,
    send_in, recv_kv, recv_qg, local_in, send_st, recv_st, send_out, recv_out, local_out,
    send_rs, recv_rs, send_ag, recv_ag, send_rim, recv_rim, tok_sem, table_sem,
):
    seg = lax.axis_index("pb")
    me = lax.axis_index("ka")
    tok = 2 * BLOCK
    n_pair = n_dev
    refs = 2 * RANDOM
    by_r = [i * RANDOM + r for r in range(RANDOM) for i in range(2)]
    seq_rows = n_dev * tok
    n_blk = 2 * n_dev

    def shift(t):
        g, r = t // 4, t % 4
        first = (3 - g) // 3
        p, q = 1 + g // 3, g // 2
        c, s = (1 - r) * (1 - r % 2), (2 - r) * (r % 2)
        along_x = first * 2 * (r % 2) + (1 - first) * (p * c - q * s)
        along_y = first * 2 * (r // 2) + (1 - first) * (p * s + q * c)
        return along_x, along_y

    my_y, my_x = me // 4, me % 4

    def peer(t):
        along_x, along_y = shift(t)
        return 4 * ((my_y + along_y + 8) % 4) + (my_x + along_x + 8) % 4

    def source(t):
        along_x, along_y = shift(t)
        return 4 * ((my_y - along_y + 8) % 4) + (my_x - along_x + 8) % 4

    def seg_peer(t):
        return lax.rem(seg + t, n_seg)

    def seg_source(t):
        return lax.rem(seg + n_seg - t, n_seg)

    def each(lo, hi, body):
        def step(t, carry):
            body(t)
            return carry

        lax.fori_loop(lo, hi, step, 0)

    def listed(d, e):
        return lax.rem(listed_at[e % RANDOM, 2 * d + e // RANDOM], n_blk)

    def arrived(ref, sem):
        pltpu.make_async_copy(ref, ref, sem).wait()

    def columns(j):
        return pl.ds(pl.multiple_of(j * DIM, DIM), DIM)

    barrier = pltpu.get_barrier_semaphore()

    def greet(t):
        pl.semaphore_signal(barrier, inc=1, device_id=(seg, peer(t)), device_id_type=MESH)

    def greet_seg(t):
        pl.semaphore_signal(barrier, inc=1, device_id=(seg_peer(t), me), device_id_type=MESH)

    each(1, n_dev, greet)
    each(1, n_seg, greet_seg)

    tok_g = pltpu.make_async_copy(grad_out, g_tok, tok_sem.at[0])
    tok_o = pltpu.make_async_copy(output, o_tok, tok_sem.at[1])
    tok_g.start()
    tok_o.start()

    inputs = (keys, values, query, grad_out)

    def landing(a, j):
        half = pl.ds((a % 2) * DIM, DIM)
        if a < 2:
            return kv.at[pl.ds(1 + 2 * j, 2), :, half]
        return qg.at[pl.ds(2 * j, 2), :, half]

    def head_in(a, j):
        return pltpu.make_async_remote_copy(
            src_ref=inputs[a].at[:, :, columns(j)],
            dst_ref=landing(a, me),
            send_sem=send_in.at[a // 2],
            recv_sem=recv_kv if a < 2 else recv_qg.at[me],
            device_id=(seg, j),
            device_id_type=MESH,
        )

    def own_in(a):
        return pltpu.make_async_copy(
            inputs[a].at[:, :, columns(me)], landing(a, me), local_in.at[a]
        )

    for a in range(4):
        own_in(a).start()

    pl.semaphore_wait(barrier, n_dev + n_seg - 2)

    def send_kv(t):
        head_in(0, peer(t)).start()
        head_in(1, peer(t)).start()

    def send_qg(t):
        head_in(2, peer(t)).start()
        head_in(3, peer(t)).start()

    each(1, n_dev, send_kv)

    tok_g.wait()
    tok_o.wait()
    lane = lax.broadcasted_iota(jnp.int32, (tok, HEADS), 1)
    delta = jnp.zeros((tok, HEADS), F32)
    for j in range(HEADS):
        part = pl.ds(j * DIM, DIM)
        product = g_tok[:, :, part].astype(F32) * o_tok[:, :, part].astype(F32)
        product = product.reshape(tok, DIM)
        delta = jnp.where(lane == j, jnp.sum(product, axis=1, keepdims=True), delta)
    lse_rows = lse_t[...].astype(F32)
    delta_t = jnp.transpose(delta.astype(BF16).astype(F32))
    for j in range(HEADS):
        stats_out[j, 0:1, :] = lse_rows[j : j + 1, :]
        stats_out[j, 1:2, :] = delta_t[j : j + 1, :]

    def stat(j):
        return pltpu.make_async_remote_copy(
            src_ref=stats_out.at[j],
            dst_ref=stats_in.at[me],
            send_sem=send_st,
            recv_sem=recv_st,
            device_id=(seg, j),
            device_id_type=MESH,
        )

    each(1, n_dev, lambda t: stat(peer(t)).start())
    stats_in[me] = stats_out[me]

    acc[...] = jnp.zeros_like(acc)
    prefix[0] = jnp.zeros_like(prefix[0])
    rim_zero = jnp.zeros((BLOCK, 2 * DIM), BF16)

    @pl.when(seg == 0)
    def _():
        kv[0] = rim_zero

    @pl.when(seg == n_seg - 1)
    def _():
        kv[n_blk + 1] = rim_zero

    block_lane = lax.broadcasted_iota(jnp.int32, (1, DIM), 1)

    def remember(t, latest):
        table[pl.ds(t, 1), :] = latest
        for k, e in enumerate(by_r):
            latest = jnp.where(block_lane == listed(source(t), e), t * refs + k + 1, latest)
        return latest

    latest = jnp.zeros((1, DIM), jnp.int32)
    table[pl.ds(n_pair, 1), :] = lax.fori_loop(0, n_pair, remember, latest)
    to_links = pltpu.make_async_copy(table, links, table_sem)
    to_links.start()

    each(1, QG_EARLY, send_qg)
    to_links.wait()

    own_in(0).wait()
    own_in(1).wait()

    arrived(kv.at[pl.ds(0, 2 * (n_dev - 1))], recv_kv)

    def rim_copy(side, src, dst, u, target):
        return pltpu.make_async_remote_copy(
            src_ref=src,
            dst_ref=dst,
            send_sem=send_rim.at[u, side],
            recv_sem=recv_rim.at[u, side],
            device_id=(target, me),
            device_id_type=MESH,
        )

    arrived(stats_in.at[pl.ds(0, n_dev - 1)], recv_st)
    kv_up = rim_copy(
        0, kv.at[n_blk], rim_kv.at[0], 0, seg_peer(1)
    )
    kv_down = rim_copy(
        1, kv.at[1], rim_kv.at[1], 0, seg_source(1)
    )
    grad_up = rim_copy(
        0, acc.at[pl.ds(BLOCK + seq_rows, BLOCK)], rim_in.at[0], 1, seg_peer(1)
    )
    grad_down = rim_copy(1, acc.at[pl.ds(0, BLOCK)], rim_in.at[1], 1, seg_source(1))
    has_next = seg < n_seg - 1
    has_prev = seg > 0

    @pl.when(has_next)
    def _():
        kv_up.start()

    @pl.when(has_prev)
    def _():
        kv_down.start()

    def scatter(u, c):
        return pltpu.make_async_remote_copy(
            src_ref=glob_x.at[u, rows(c, 8)],
            dst_ref=glob_rs.at[u, seg],
            send_sem=send_rs.at[u],
            recv_sem=recv_rs.at[u],
            device_id=(c, me),
            device_id_type=MESH,
        )

    def spread(u, c):
        return pltpu.make_async_remote_copy(
            src_ref=glob_red.at[u],
            dst_ref=glob_y.at[u, rows(seg, 8)],
            send_sem=send_ag.at[u],
            recv_sem=recv_ag.at[u],
            device_id=(c, me),
            device_id_type=MESH,
        )

    others = pl.ds(0, n_seg - 1)
    others_rows = pl.ds(0, 8 * (n_seg - 1))

    def sum_start(u):
        each(1, n_seg, lambda t: scatter(u, seg_peer(t)).start())

    def sum_middle(u):
        arrived(glob_rs.at[u, others], recv_rs.at[u])
        total = glob_x[u, rows(seg, 8), :]
        for t in range(1, n_seg):
            total += glob_rs[u, seg_source(t)]
        glob_red[u] = total
        glob_y[u, rows(seg, 8), :] = total
        each(1, n_seg, lambda t: spread(u, seg_peer(t)).start())

    def sum_end(u):
        arrived(glob_y.at[u, others_rows], recv_ag.at[u])

    def sum_drain(u):
        arrived(glob_rs.at[u, others], send_rs.at[u])
        arrived(glob_y.at[u, others_rows], send_ag.at[u])

    def key_block(at):
        return kv[at + 1]

    def owned(i):
        return jnp.where(glob_id[i] // n_blk == seg, 1.0, 0.0).astype(F32)

    for i in range(GLOBAL):
        glob_x[0, pl.ds(i * BLOCK, BLOCK), :] = (
            key_block(lax.rem(glob_id[i], n_blk)).astype(F32) * owned(i)
        )
    sum_start(0)
    each(QG_EARLY, QG_MIDDLE, send_qg)
    glob_x[1] = jnp.zeros((GLOBAL * BLOCK, 2 * DIM), F32)

    def out_copy(a, j):
        out, held = ((dq_hbm, dq_out), (dk_hbm, dk_out), (dv_hbm, dv_out))[a]
        return pltpu.make_async_remote_copy(
            src_ref=held.at[rows(j, tok)],
            dst_ref=out.at[:, columns(me)],
            send_sem=send_out.at[a],
            recv_sem=recv_out.at[a],
            device_id=(seg, j),
            device_id_type=MESH,
        )

    def own_out(a):
        out, held = ((dq_hbm, dq_out), (dk_hbm, dk_out), (dv_hbm, dv_out))[a]
        return pltpu.make_async_copy(
            held.at[rows(me, tok)], out.at[:, columns(me)], local_out.at[a]
        )

    lane = lax.broadcasted_iota(jnp.int32, (1, 2 * DIM), 1)
    scale = jnp.where(lane < DIM, 1.0, FACTOR).astype(F32)

    def pair(d):
        both = qg[pl.ds(2 * d, 2)].reshape(tok, 2 * DIM)
        q = both[:, :DIM]
        g = both[:, DIM:]
        lse = stats_in[d, 0:1, :]
        row_delta = stats_in[d, 1:2, :]
        zero = jnp.zeros((tok, DIM), BF16)
        into = jnp.concatenate(
            [jnp.concatenate([q, zero], 1), jnp.concatenate([zero, g], 1)], 0
        )
        back = jnp.concatenate(
            [jnp.concatenate([g, zero], 1), jnp.concatenate([zero, q], 1)], 0
        )

        def entries(block, active):
            both = lax.dot_general(
                block, into, (((1,), (1,)), ((), ())), preferred_element_type=F32
            )
            weights = jnp.exp(both[:, :DIM] * FACTOR - lse)
            if active is not None:
                weights = jnp.where(active, weights, 0.0)
            dscore = (weights * (both[:, DIM:] - row_delta)).astype(BF16)
            grads = jnp.dot(
                jnp.concatenate([weights.astype(BF16), dscore], 1),
                back,
                preferred_element_type=F32,
            )
            return grads * scale, dscore

        return entries

    def query_grad(dscore, block):
        return FACTOR * lax.dot_general(
            dscore, block[:, :DIM], (((0,), (0,)), ((), ())), preferred_element_type=F32
        )

    def places(count):
        key_at = lax.broadcasted_iota(jnp.int32, (count, tok), 0)
        query_at = lax.broadcasted_iota(jnp.int32, (count, tok), 1) // BLOCK
        return key_at // BLOCK, query_at

    def send_dq(t):
        d = source(t)

        @pl.when(t == 0)
        def _():
            own_out(0).start()

        @pl.when(t > 0)
        def _():
            out_copy(0, d).start()

    win, rand = 4 * BLOCK, 2 * BLOCK

    def wait_rows(t):
        d = source(t)

        @pl.when(t == 0)
        def _():
            own_in(2).wait()
            own_in(3).wait()

        @pl.when(t > 0)
        def _():
            arrived(qg.at[pl.ds(2 * d, 2)], recv_qg.at[d])

    def pair_part(t, late):
        d = source(t)

        @pl.when((d == 0) & has_prev)
        def _():
            kv_up.wait_recv()
            kv[0] = rim_kv[0]

        @pl.when((d == n_pair - 1) & has_next)
        def _():
            kv_down.wait_recv()
            kv[n_blk + 1] = rim_kv[1]

        key_at, query_at = places(win)
        absolute = seg * n_blk + 2 * d - 1 + key_at
        near = (
            (key_at >= query_at)
            & (key_at <= query_at + 2)
            & (absolute >= 0)
            & (absolute < n_seg * n_blk)
        )
        key_at, query_at = places(rand)
        own = key_at == query_at
        found = [listed(d, e) for e in by_r]
        block = jnp.concatenate(
            [kv[pl.ds(2 * d, 4)].reshape(win, 2 * DIM)] + [key_block(b) for b in found], 0
        )
        grads, dscore = pair(d)(block, jnp.concatenate([near] + [own] * RANDOM, 0))
        above = pl.ds(pl.multiple_of(d * tok, tok), BLOCK)
        inside = pl.ds(pl.multiple_of(d * tok + BLOCK, BLOCK), tok)
        below = pl.ds(pl.multiple_of(d * tok + BLOCK + tok, BLOCK), BLOCK)
        acc[above, :] += rounded(grads[:BLOCK])
        acc[inside, :] += grads[BLOCK : BLOCK + tok]
        acc[below, :] += rounded(grads[BLOCK + tok : win])
        dq = query_grad(dscore[:win], block[:win])
        if late:
            dq += dq_acc[rows(d, tok), :]
        for r in range(RANDOM):
            part = slice(win + r * rand, win + (r + 1) * rand)
            dq += rounded(query_grad(dscore[part], block[part]))
        if late:
            dq_out[rows(d, tok), :] = dq.astype(BF16)
        else:
            dq_acc[rows(d, tok), :] = dq
        for k, b in enumerate(found):
            at = win + k * BLOCK
            prefix[t * refs + k + 1] = rounded(grads[at : at + BLOCK]) + prefix[links[t, b]]

    def global_part(t, late):
        d = source(t)
        block = glob_kv[...]
        grads, dscore = pair(d)(block, None)
        glob_x[1] += grads
        dq = query_grad(dscore, block)
        if late:
            dq_acc[rows(d, tok), :] = dq
        else:
            dq_out[rows(d, tok), :] = (dq + dq_acc[rows(d, tok), :]).astype(BF16)

    half = n_pair // 2

    def early(t):
        wait_rows(t)
        pair_part(t, False)

    def globals_of(t):
        wait_rows(t)
        global_part(t, True)
        global_part(t - half, False)

    def late(t):
        pair_part(t, True)
        send_dq(t)

    each(0, n_pair // 4, early)
    sum_middle(0)
    each(QG_MIDDLE, n_dev, send_qg)
    each(n_pair // 4, half, early)
    sum_end(0)
    glob_kv[...] = glob_y[0].astype(BF16)
    each(half, n_pair, globals_of)

    sum_start(1)
    each(0, half, send_dq)
    each(half, LATE, late)
    sum_middle(1)
    each(LATE, n_pair, late)

    @pl.when(has_next)
    def _():
        grad_up.start()

    @pl.when(has_prev)
    def _():
        grad_down.start()

    @pl.when(has_prev)
    def _():
        grad_up.wait_recv()
        acc[pl.ds(BLOCK, BLOCK), :] += rim_in[0]

    @pl.when(has_next)
    def _():
        grad_down.wait_recv()
        acc[pl.ds(seq_rows, BLOCK), :] += rim_in[1]

    sum_end(1)

    def finish(t):
        d = source(t)
        for i in range(2):
            b = 2 * d + i
            at = pl.ds(pl.multiple_of(b * BLOCK, BLOCK), BLOCK)
            total = acc[pl.ds(pl.multiple_of(BLOCK + b * BLOCK, BLOCK), BLOCK), :]
            total += prefix[links[n_pair, b]]
            for j in range(GLOBAL):
                here = jnp.where(glob_id[j] == seg * n_blk + b, 1.0, 0.0).astype(F32)
                total += glob_y[1, pl.ds(j * BLOCK, BLOCK), :] * here
            dv_out[at, :] = total[:, :DIM].astype(BF16)
            dk_out[at, :] = total[:, DIM:].astype(BF16)

        @pl.when(t == 0)
        def _():
            own_out(1).start()
            own_out(2).start()

        @pl.when(t > 0)
        def _():
            out_copy(1, d).start()
            out_copy(2, d).start()

    each(0, n_pair, finish)

    sum_drain(0)
    sum_drain(1)

    @pl.when(has_next)
    def _():
        kv_up.wait_send()
        grad_up.wait_send()

    @pl.when(has_prev)
    def _():
        kv_down.wait_send()
        grad_down.wait_send()

    most = pl.ds(0, 2 * (n_dev - 1))
    arrived(kv.at[most], send_in.at[0])
    arrived(qg.at[most], send_in.at[1])
    arrived(stats_out.at[pl.ds(0, n_dev - 1)], send_st)
    for a, (out, held) in enumerate(((dq_hbm, dq_out), (dk_hbm, dk_out), (dv_hbm, dv_out))):
        arrived(held.at[pl.ds(0, (n_dev - 1) * tok)], send_out.at[a])
        own_out(a).wait()
        arrived(out.at[:, pl.ds(0, (n_dev - 1) * DIM)], recv_out.at[a])


def shards(query, keys, values, output, grad_out, log_sum_exp, random_blocks, global_blocks):
    tok, width = query.shape
    query, keys, values, output, grad_out = (
        x.reshape(2, BLOCK, width) for x in (query, keys, values, output, grad_out)
    )
    n_seg, n_dev = lax.axis_size("pb"), lax.axis_size("ka")
    refs = 2 * RANDOM
    n_blk = 2 * n_dev
    count = n_dev * refs

    smem = pl.BlockSpec(memory_space=pltpu.SMEM)
    hbm = pl.BlockSpec(memory_space=pltpu.HBM)
    vmem = pl.BlockSpec(memory_space=pltpu.VMEM)
    dma = pltpu.SemaphoreType.DMA
    seq = n_dev * tok
    glob = GLOBAL * BLOCK
    out = jax.ShapeDtypeStruct((tok, width), BF16)
    grads = pl.pallas_call(
        functools.partial(kernel, n_seg, n_dev),
        out_shape=(out, out, out),
        in_specs=[smem, smem, hbm, hbm, hbm, hbm, hbm, vmem],
        out_specs=(hbm, hbm, hbm),
        scratch_shapes=[
            pltpu.VMEM((n_blk + 2, BLOCK, 2 * DIM), BF16),
            pltpu.VMEM((n_blk, BLOCK, 2 * DIM), BF16),
            pltpu.VMEM((seq + 2 * BLOCK, 2 * DIM), F32),
            pltpu.VMEM((count + 1, BLOCK, 2 * DIM), F32),
            pltpu.VMEM((seq, DIM), F32),
            pltpu.VMEM((seq, DIM), BF16),
            pltpu.VMEM((seq, DIM), BF16),
            pltpu.VMEM((seq, DIM), BF16),
            pltpu.VMEM((2, BLOCK, width), BF16),
            pltpu.VMEM((2, BLOCK, width), BF16),
            pltpu.VMEM((n_dev, 8, tok), F32),
            pltpu.VMEM((n_dev, 8, tok), F32),
            pltpu.VMEM((2, glob, 2 * DIM), F32),
            pltpu.VMEM((2, n_seg, 8, 2 * DIM), F32),
            pltpu.VMEM((2, 8, 2 * DIM), F32),
            pltpu.VMEM((2, glob, 2 * DIM), F32),
            pltpu.VMEM((glob, 2 * DIM), BF16),
            pltpu.VMEM((2, BLOCK, 2 * DIM), BF16),
            pltpu.VMEM((2, BLOCK, 2 * DIM), F32),
            pltpu.VMEM((n_dev + 8, DIM), jnp.int32),
            pltpu.SMEM((n_dev + 8, DIM), jnp.int32),
            dma((2,)),
            dma(()),
            dma((n_dev,)),
            dma((4,)),
            dma(()),
            dma(()),
            dma((3,)),
            dma((3,)),
            dma((3,)),
            dma((2,)),
            dma((2,)),
            dma((2,)),
            dma((2,)),
            dma((2, 2)),
            dma((2, 2)),
            dma((2,)),
            dma(()),
        ],
        compiler_params=pltpu.CompilerParams(
            collective_id=0, has_side_effects=True, vmem_limit_bytes=52 * 2**20
        ),
        cost_estimate=pl.CostEstimate(
            flops=2**32, bytes_accessed=2**23, transcendentals=2**21
        ),
    )(jnp.transpose(random_blocks), global_blocks, query, keys, values, output, grad_out, jnp.transpose(log_sum_exp))
    return grads


def solution(mesh):
    both = P(("pb", "ka"), None)
    return jax.shard_map(
        shards,
        mesh=mesh,
        in_specs=(both, both, both, both, both, both, P("pb", None), P()),
        out_specs=(both, both, both),
        check_vma=False,
    )
```

```python
import functools

import jax
import jax.numpy as jnp
from jax import lax
from jax.experimental import pallas as pl
from jax.experimental.pallas import tpu as pltpu
from jax.sharding import PartitionSpec as P

HEADS = 16
DIM = 128
BLOCK = 64
RANDOM = 3
GLOBAL = 2
QG_EARLY = 4
QG_MIDDLE = 12
LATE = 14
MESH = pl.DeviceIdType.MESH
F32 = jnp.float32
BF16 = jnp.bfloat16
FACTOR = DIM**-0.5


def rows(index, size):
    return pl.ds(pl.multiple_of(index * size, size), size)


def rounded(value):
    return value.astype(BF16).astype(F32)


def kernel(
    n_seg, n_dev,
    listed_at, glob_id, query, keys, values, output, grad_out, lse_t,
    dq_hbm, dk_hbm, dv_hbm,
    kv, qg, acc, prefix, dq_acc, dq_out, dk_out, dv_out, g_tok, o_tok, stats_out, stats_in,
    glob_x, glob_rs, glob_red, glob_y, glob_kv, rim_kv, rim_in, table, links,
    send_in, recv_kv, recv_qg, local_in, send_st, recv_st, send_out, recv_out, local_out,
    send_rs, recv_rs, send_ag, recv_ag, send_rim, recv_rim, tok_sem, table_sem,
):
    seg = lax.axis_index("pb")
    me = lax.axis_index("ka")
    tok = 2 * BLOCK
    n_pair = n_dev
    refs = 2 * RANDOM
    by_r = [i * RANDOM + r for r in range(RANDOM) for i in range(2)]
    seq_rows = n_dev * tok
    n_blk = 2 * n_dev

    def shift(t):
        g, r = t // 4, t % 4
        first = (3 - g) // 3
        p, q = 1 + g // 3, g // 2
        c, s = (1 - r) * (1 - r % 2), (2 - r) * (r % 2)
        along_x = first * 2 * (r % 2) + (1 - first) * (p * c - q * s)
        along_y = first * 2 * (r // 2) + (1 - first) * (p * s + q * c)
        return along_x, along_y

    my_y, my_x = me // 4, me % 4

    def peer(t):
        along_x, along_y = shift(t)
        return 4 * ((my_y + along_y + 8) % 4) + (my_x + along_x + 8) % 4

    def source(t):
        along_x, along_y = shift(t)
        return 4 * ((my_y - along_y + 8) % 4) + (my_x - along_x + 8) % 4

    def seg_peer(t):
        return lax.rem(seg + t, n_seg)

    def seg_far_first(t):
        away = n_seg // 2 + (2 * (t % 2) - 1) * (t // 2)
        return lax.rem(seg + away, n_seg)

    def seg_source(t):
        return lax.rem(seg + n_seg - t, n_seg)

    def each(lo, hi, body):
        def step(t, carry):
            body(t)
            return carry

        lax.fori_loop(lo, hi, step, 0)

    def listed(d, e):
        return lax.rem(listed_at[e % RANDOM, 2 * d + e // RANDOM], n_blk)

    def arrived(ref, sem):
        pltpu.make_async_copy(ref, ref, sem).wait()

    def columns(j):
        return pl.ds(pl.multiple_of(j * DIM, DIM), DIM)

    barrier = pltpu.get_barrier_semaphore()

    def greet(t):
        pl.semaphore_signal(barrier, inc=1, device_id=(seg, peer(t)), device_id_type=MESH)

    def greet_seg(t):
        pl.semaphore_signal(barrier, inc=1, device_id=(seg_peer(t), me), device_id_type=MESH)

    each(1, n_dev, greet)
    each(1, n_seg, greet_seg)

    tok_g = pltpu.make_async_copy(grad_out, g_tok, tok_sem.at[0])
    tok_o = pltpu.make_async_copy(output, o_tok, tok_sem.at[1])
    tok_g.start()
    tok_o.start()

    inputs = (keys, values, query, grad_out)

    def landing(a, j):
        half = pl.ds((a % 2) * DIM, DIM)
        if a < 2:
            return kv.at[pl.ds(1 + 2 * j, 2), :, half]
        return qg.at[pl.ds(2 * j, 2), :, half]

    def head_in(a, j):
        return pltpu.make_async_remote_copy(
            src_ref=inputs[a].at[:, :, columns(j)],
            dst_ref=landing(a, me),
            send_sem=send_in.at[a // 2],
            recv_sem=recv_kv if a < 2 else recv_qg.at[me],
            device_id=(seg, j),
            device_id_type=MESH,
        )

    def own_in(a):
        return pltpu.make_async_copy(
            inputs[a].at[:, :, columns(me)], landing(a, me), local_in.at[a]
        )

    for a in range(4):
        own_in(a).start()

    pl.semaphore_wait(barrier, n_dev + n_seg - 2)

    def send_kv(t):
        head_in(0, peer(t)).start()
        head_in(1, peer(t)).start()

    def send_qg(t):
        head_in(2, peer(t)).start()
        head_in(3, peer(t)).start()

    each(1, n_dev, lambda t: send_kv(n_dev - t))

    tok_g.wait()
    tok_o.wait()
    lane = lax.broadcasted_iota(jnp.int32, (tok, HEADS), 1)
    delta = jnp.zeros((tok, HEADS), F32)
    for j in range(HEADS):
        part = pl.ds(j * DIM, DIM)
        product = g_tok[:, :, part].astype(F32) * o_tok[:, :, part].astype(F32)
        product = product.reshape(tok, DIM)
        delta = jnp.where(lane == j, jnp.sum(product, axis=1, keepdims=True), delta)
    lse_rows = lse_t[...].astype(F32)
    delta_t = jnp.transpose(delta.astype(BF16).astype(F32))
    for j in range(HEADS):
        stats_out[j, 0:1, :] = lse_rows[j : j + 1, :]
        stats_out[j, 1:2, :] = delta_t[j : j + 1, :]

    def stat(j):
        return pltpu.make_async_remote_copy(
            src_ref=stats_out.at[j],
            dst_ref=stats_in.at[me],
            send_sem=send_st,
            recv_sem=recv_st,
            device_id=(seg, j),
            device_id_type=MESH,
        )

    each(1, n_dev, lambda t: stat(peer(t)).start())
    stats_in[me] = stats_out[me]

    acc[...] = jnp.zeros_like(acc)
    prefix[0] = jnp.zeros_like(prefix[0])
    rim_zero = jnp.zeros((BLOCK, 2 * DIM), BF16)

    @pl.when(seg == 0)
    def _():
        kv[0] = rim_zero

    @pl.when(seg == n_seg - 1)
    def _():
        kv[n_blk + 1] = rim_zero

    block_lane = lax.broadcasted_iota(jnp.int32, (1, DIM), 1)

    def remember(t, latest):
        table[pl.ds(t, 1), :] = latest
        for k, e in enumerate(by_r):
            latest = jnp.where(block_lane == listed(source(t), e), t * refs + k + 1, latest)
        return latest

    latest = jnp.zeros((1, DIM), jnp.int32)
    table[pl.ds(n_pair, 1), :] = lax.fori_loop(0, n_pair, remember, latest)
    to_links = pltpu.make_async_copy(table, links, table_sem)
    to_links.start()

    each(1, QG_EARLY, send_qg)
    to_links.wait()

    own_in(0).wait()
    own_in(1).wait()

    arrived(kv.at[pl.ds(0, 2 * (n_dev - 1))], recv_kv)

    def rim_copy(side, src, dst, u, target):
        return pltpu.make_async_remote_copy(
            src_ref=src,
            dst_ref=dst,
            send_sem=send_rim.at[u, side],
            recv_sem=recv_rim.at[u, side],
            device_id=(target, me),
            device_id_type=MESH,
        )

    arrived(stats_in.at[pl.ds(0, n_dev - 1)], recv_st)
    kv_up = rim_copy(
        0, kv.at[n_blk], rim_kv.at[0], 0, seg_peer(1)
    )
    kv_down = rim_copy(
        1, kv.at[1], rim_kv.at[1], 0, seg_source(1)
    )
    grad_up = rim_copy(
        0, acc.at[pl.ds(BLOCK + seq_rows, BLOCK)], rim_in.at[0], 1, seg_peer(1)
    )
    grad_down = rim_copy(1, acc.at[pl.ds(0, BLOCK)], rim_in.at[1], 1, seg_source(1))
    has_next = seg < n_seg - 1
    has_prev = seg > 0

    @pl.when(has_next)
    def _():
        kv_up.start()

    @pl.when(has_prev)
    def _():
        kv_down.start()

    def scatter(u, c):
        return pltpu.make_async_remote_copy(
            src_ref=glob_x.at[u, rows(c, 8)],
            dst_ref=glob_rs.at[u, seg],
            send_sem=send_rs.at[u],
            recv_sem=recv_rs.at[u],
            device_id=(c, me),
            device_id_type=MESH,
        )

    def spread(u, c):
        return pltpu.make_async_remote_copy(
            src_ref=glob_red.at[u],
            dst_ref=glob_y.at[u, rows(seg, 8)],
            send_sem=send_ag.at[u],
            recv_sem=recv_ag.at[u],
            device_id=(c, me),
            device_id_type=MESH,
        )

    others = pl.ds(0, n_seg - 1)
    others_rows = pl.ds(0, 8 * (n_seg - 1))

    def sum_start(u):
        each(1, n_seg, lambda t: scatter(u, seg_far_first(t)).start())

    def sum_middle(u):
        arrived(glob_rs.at[u, others], recv_rs.at[u])
        total = glob_x[u, rows(seg, 8), :]
        for t in range(1, n_seg):
            total += glob_rs[u, seg_source(t)]
        glob_red[u] = total
        glob_y[u, rows(seg, 8), :] = total
        each(1, n_seg, lambda t: spread(u, seg_far_first(t)).start())

    def sum_end(u):
        arrived(glob_y.at[u, others_rows], recv_ag.at[u])

    def sum_drain(u):
        arrived(glob_rs.at[u, others], send_rs.at[u])
        arrived(glob_y.at[u, others_rows], send_ag.at[u])

    def key_block(at):
        return kv[at + 1]

    def owned(i):
        return jnp.where(glob_id[i] // n_blk == seg, 1.0, 0.0).astype(F32)

    for i in range(GLOBAL):
        glob_x[0, pl.ds(i * BLOCK, BLOCK), :] = (
            key_block(lax.rem(glob_id[i], n_blk)).astype(F32) * owned(i)
        )
    sum_start(0)
    each(QG_EARLY, QG_MIDDLE, send_qg)
    glob_x[1] = jnp.zeros((GLOBAL * BLOCK, 2 * DIM), F32)

    def out_copy(a, j):
        out, held = ((dq_hbm, dq_out), (dk_hbm, dk_out), (dv_hbm, dv_out))[a]
        return pltpu.make_async_remote_copy(
            src_ref=held.at[rows(j, tok)],
            dst_ref=out.at[:, columns(me)],
            send_sem=send_out.at[a],
            recv_sem=recv_out.at[a],
            device_id=(seg, j),
            device_id_type=MESH,
        )

    def own_out(a):
        out, held = ((dq_hbm, dq_out), (dk_hbm, dk_out), (dv_hbm, dv_out))[a]
        return pltpu.make_async_copy(
            held.at[rows(me, tok)], out.at[:, columns(me)], local_out.at[a]
        )

    lane = lax.broadcasted_iota(jnp.int32, (1, 2 * DIM), 1)
    scale = jnp.where(lane < DIM, 1.0, FACTOR).astype(F32)

    def pair(d):
        both = qg[pl.ds(2 * d, 2)].reshape(tok, 2 * DIM)
        q = both[:, :DIM]
        g = both[:, DIM:]
        lse = stats_in[d, 0:1, :]
        row_delta = stats_in[d, 1:2, :]
        zero = jnp.zeros((tok, DIM), BF16)
        into = jnp.concatenate(
            [jnp.concatenate([q, zero], 1), jnp.concatenate([zero, g], 1)], 0
        )
        back = jnp.concatenate(
            [jnp.concatenate([g, zero], 1), jnp.concatenate([zero, q], 1)], 0
        )

        def entries(block, active):
            both = lax.dot_general(
                block, into, (((1,), (1,)), ((), ())), preferred_element_type=F32
            )
            weights = jnp.exp(both[:, :DIM] * FACTOR - lse)
            if active is not None:
                weights = jnp.where(active, weights, 0.0)
            dscore = (weights * (both[:, DIM:] - row_delta)).astype(BF16)
            grads = jnp.dot(
                jnp.concatenate([weights.astype(BF16), dscore], 1),
                back,
                preferred_element_type=F32,
            )
            return grads * scale, dscore

        return entries

    def query_grad(dscore, block):
        return FACTOR * lax.dot_general(
            dscore, block[:, :DIM], (((0,), (0,)), ((), ())), preferred_element_type=F32
        )

    def places(count):
        key_at = lax.broadcasted_iota(jnp.int32, (count, tok), 0)
        query_at = lax.broadcasted_iota(jnp.int32, (count, tok), 1) // BLOCK
        return key_at // BLOCK, query_at

    def send_dq(t):
        d = source(t)

        @pl.when(t == 0)
        def _():
            own_out(0).start()

        @pl.when(t > 0)
        def _():
            out_copy(0, d).start()

    win, rand = 4 * BLOCK, 2 * BLOCK

    def wait_rows(t):
        d = source(t)

        @pl.when(t == 0)
        def _():
            own_in(2).wait()
            own_in(3).wait()

        @pl.when(t > 0)
        def _():
            arrived(qg.at[pl.ds(2 * d, 2)], recv_qg.at[d])

    def pair_part(t, late):
        d = source(t)

        @pl.when((d == 0) & has_prev)
        def _():
            kv_up.wait_recv()
            kv[0] = rim_kv[0]

        @pl.when((d == n_pair - 1) & has_next)
        def _():
            kv_down.wait_recv()
            kv[n_blk + 1] = rim_kv[1]

        key_at, query_at = places(win)
        absolute = seg * n_blk + 2 * d - 1 + key_at
        near = (
            (key_at >= query_at)
            & (key_at <= query_at + 2)
            & (absolute >= 0)
            & (absolute < n_seg * n_blk)
        )
        key_at, query_at = places(rand)
        own = key_at == query_at
        found = [listed(d, e) for e in by_r]
        block = jnp.concatenate(
            [kv[pl.ds(2 * d, 4)].reshape(win, 2 * DIM)] + [key_block(b) for b in found], 0
        )
        grads, dscore = pair(d)(block, jnp.concatenate([near] + [own] * RANDOM, 0))
        above = pl.ds(pl.multiple_of(d * tok, tok), BLOCK)
        inside = pl.ds(pl.multiple_of(d * tok + BLOCK, BLOCK), tok)
        below = pl.ds(pl.multiple_of(d * tok + BLOCK + tok, BLOCK), BLOCK)
        acc[above, :] += rounded(grads[:BLOCK])
        acc[inside, :] += grads[BLOCK : BLOCK + tok]
        acc[below, :] += rounded(grads[BLOCK + tok : win])
        dq = query_grad(dscore[:win], block[:win])
        if late:
            dq += dq_acc[rows(d, tok), :]
        for r in range(RANDOM):
            part = slice(win + r * rand, win + (r + 1) * rand)
            dq += rounded(query_grad(dscore[part], block[part]))
        if late:
            dq_out[rows(d, tok), :] = dq.astype(BF16)
        else:
            dq_acc[rows(d, tok), :] = dq
        for k, b in enumerate(found):
            at = win + k * BLOCK
            prefix[t * refs + k + 1] = rounded(grads[at : at + BLOCK]) + prefix[links[t, b]]

    def global_part(t, late):
        d = source(t)
        block = glob_kv[...]
        grads, dscore = pair(d)(block, None)
        glob_x[1] += grads
        dq = query_grad(dscore, block)
        if late:
            dq_acc[rows(d, tok), :] = dq
        else:
            dq_out[rows(d, tok), :] = (dq + dq_acc[rows(d, tok), :]).astype(BF16)

    half = n_pair // 2

    def early(t):
        wait_rows(t)
        pair_part(t, False)

    def globals_of(t):
        wait_rows(t)
        global_part(t, True)
        global_part(t - half, False)

    def late(t):
        pair_part(t, True)
        send_dq(t)

    each(0, 2, early)
    sum_middle(0)
    each(QG_MIDDLE, n_dev, send_qg)
    each(2, half, early)
    sum_end(0)
    glob_kv[...] = glob_y[0].astype(BF16)
    each(half, n_pair, globals_of)

    sum_start(1)
    each(0, half, send_dq)
    each(half, LATE, late)
    sum_middle(1)
    each(LATE, n_pair, late)

    @pl.when(has_next)
    def _():
        grad_up.start()

    @pl.when(has_prev)
    def _():
        grad_down.start()

    @pl.when(has_prev)
    def _():
        grad_up.wait_recv()
        acc[pl.ds(BLOCK, BLOCK), :] += rim_in[0]

    @pl.when(has_next)
    def _():
        grad_down.wait_recv()
        acc[pl.ds(seq_rows, BLOCK), :] += rim_in[1]

    sum_end(1)

    def finish(t):
        d = source(t)
        for i in range(2):
            b = 2 * d + i
            at = pl.ds(pl.multiple_of(b * BLOCK, BLOCK), BLOCK)
            total = acc[pl.ds(pl.multiple_of(BLOCK + b * BLOCK, BLOCK), BLOCK), :]
            total += prefix[links[n_pair, b]]
            for j in range(GLOBAL):
                here = jnp.where(glob_id[j] == seg * n_blk + b, 1.0, 0.0).astype(F32)
                total += glob_y[1, pl.ds(j * BLOCK, BLOCK), :] * here
            dv_out[at, :] = total[:, :DIM].astype(BF16)
            dk_out[at, :] = total[:, DIM:].astype(BF16)

        @pl.when(t == 0)
        def _():
            own_out(1).start()
            own_out(2).start()

        @pl.when(t > 0)
        def _():
            out_copy(1, d).start()
            out_copy(2, d).start()

    each(0, n_pair, lambda t: finish(n_pair - 1 - t))

    sum_drain(0)
    sum_drain(1)

    @pl.when(has_next)
    def _():
        kv_up.wait_send()
        grad_up.wait_send()

    @pl.when(has_prev)
    def _():
        kv_down.wait_send()
        grad_down.wait_send()

    most = pl.ds(0, 2 * (n_dev - 1))
    arrived(kv.at[most], send_in.at[0])
    arrived(qg.at[most], send_in.at[1])
    arrived(stats_out.at[pl.ds(0, n_dev - 1)], send_st)
    for a, (out, held) in enumerate(((dq_hbm, dq_out), (dk_hbm, dk_out), (dv_hbm, dv_out))):
        arrived(held.at[pl.ds(0, (n_dev - 1) * tok)], send_out.at[a])
        own_out(a).wait()
        arrived(out.at[:, pl.ds(0, (n_dev - 1) * DIM)], recv_out.at[a])


def shards(query, keys, values, output, grad_out, log_sum_exp, random_blocks, global_blocks):
    tok, width = query.shape
    query, keys, values, output, grad_out = (
        x.reshape(2, BLOCK, width) for x in (query, keys, values, output, grad_out)
    )
    n_seg, n_dev = lax.axis_size("pb"), lax.axis_size("ka")
    refs = 2 * RANDOM
    n_blk = 2 * n_dev
    count = n_dev * refs

    smem = pl.BlockSpec(memory_space=pltpu.SMEM)
    hbm = pl.BlockSpec(memory_space=pltpu.HBM)
    vmem = pl.BlockSpec(memory_space=pltpu.VMEM)
    dma = pltpu.SemaphoreType.DMA
    seq = n_dev * tok
    glob = GLOBAL * BLOCK
    out = jax.ShapeDtypeStruct((tok, width), BF16)
    grads = pl.pallas_call(
        functools.partial(kernel, n_seg, n_dev),
        out_shape=(out, out, out),
        in_specs=[smem, smem, hbm, hbm, hbm, hbm, hbm, vmem],
        out_specs=(hbm, hbm, hbm),
        scratch_shapes=[
            pltpu.VMEM((n_blk + 2, BLOCK, 2 * DIM), BF16),
            pltpu.VMEM((n_blk, BLOCK, 2 * DIM), BF16),
            pltpu.VMEM((seq + 2 * BLOCK, 2 * DIM), F32),
            pltpu.VMEM((count + 1, BLOCK, 2 * DIM), F32),
            pltpu.VMEM((seq, DIM), F32),
            pltpu.VMEM((seq, DIM), BF16),
            pltpu.VMEM((seq, DIM), BF16),
            pltpu.VMEM((seq, DIM), BF16),
            pltpu.VMEM((2, BLOCK, width), BF16),
            pltpu.VMEM((2, BLOCK, width), BF16),
            pltpu.VMEM((n_dev, 8, tok), F32),
            pltpu.VMEM((n_dev, 8, tok), F32),
            pltpu.VMEM((2, glob, 2 * DIM), F32),
            pltpu.VMEM((2, n_seg, 8, 2 * DIM), F32),
            pltpu.VMEM((2, 8, 2 * DIM), F32),
            pltpu.VMEM((2, glob, 2 * DIM), F32),
            pltpu.VMEM((glob, 2 * DIM), BF16),
            pltpu.VMEM((2, BLOCK, 2 * DIM), BF16),
            pltpu.VMEM((2, BLOCK, 2 * DIM), F32),
            pltpu.VMEM((n_dev + 8, DIM), jnp.int32),
            pltpu.SMEM((n_dev + 8, DIM), jnp.int32),
            dma((2,)),
            dma(()),
            dma((n_dev,)),
            dma((4,)),
            dma(()),
            dma(()),
            dma((3,)),
            dma((3,)),
            dma((3,)),
            dma((2,)),
            dma((2,)),
            dma((2,)),
            dma((2,)),
            dma((2, 2)),
            dma((2, 2)),
            dma((2,)),
            dma(()),
        ],
        compiler_params=pltpu.CompilerParams(
            collective_id=0, has_side_effects=True, vmem_limit_bytes=52 * 2**20
        ),
        cost_estimate=pl.CostEstimate(
            flops=2**32, bytes_accessed=2**23, transcendentals=2**21
        ),
    )(jnp.transpose(random_blocks), global_blocks, query, keys, values, output, grad_out, jnp.transpose(log_sum_exp))
    return grads


def solution(mesh):
    both = P(("pb", "ka"), None)
    return jax.shard_map(
        shards,
        mesh=mesh,
        in_specs=(both, both, both, both, both, both, P("pb", None), P()),
        out_specs=(both, both, both),
        check_vma=False,
    )
```

```python
import functools

import jax
import jax.numpy as jnp
from jax import lax
from jax.experimental import pallas as pl
from jax.experimental.pallas import tpu as pltpu
from jax.sharding import PartitionSpec as P

HEADS = 16
DIM = 128
BLOCK = 64
RANDOM = 3
GLOBAL = 2
QG_EARLY = 4
QG_MIDDLE = 12
LATE = 14
MESH = pl.DeviceIdType.MESH
F32 = jnp.float32
BF16 = jnp.bfloat16
FACTOR = DIM**-0.5


def rows(index, size):
    return pl.ds(pl.multiple_of(index * size, size), size)


def rounded(value):
    return value.astype(BF16).astype(F32)


def kernel(
    n_seg, n_dev,
    listed_at, glob_id, query, keys, values, output, grad_out, lse_t,
    dq_hbm, dk_hbm, dv_hbm,
    kv, qg, acc, prefix, dq_acc, dq_out, dk_out, dv_out, g_tok, o_tok, stats_out, stats_in,
    glob_x, glob_rs, glob_red, glob_y, glob_kv, rim_kv, rim_in, table, links,
    send_in, recv_kv, recv_qg, local_in, send_st, recv_st, send_out, recv_out, local_out,
    send_rs, recv_rs, send_ag, recv_ag, send_rim, recv_rim, tok_sem, table_sem,
):
    seg = lax.axis_index("pb")
    me = lax.axis_index("ka")
    tok = 2 * BLOCK
    n_pair = n_dev
    refs = 2 * RANDOM
    by_r = [i * RANDOM + r for r in range(RANDOM) for i in range(2)]
    seq_rows = n_dev * tok
    n_blk = 2 * n_dev

    def shift(t):
        g, r = t // 4, t % 4
        first = (3 - g) // 3
        p, q = 1 + g // 3, g // 2
        c, s = (1 - r) * (1 - r % 2), (2 - r) * (r % 2)
        along_x = first * 2 * (r % 2) + (1 - first) * (p * c - q * s)
        along_y = first * 2 * (r // 2) + (1 - first) * (p * s + q * c)
        return along_x, along_y

    my_y, my_x = me // 4, me % 4

    def peer(t):
        along_x, along_y = shift(t)
        return 4 * ((my_y + along_y + 8) % 4) + (my_x + along_x + 8) % 4

    def source(t):
        along_x, along_y = shift(t)
        return 4 * ((my_y - along_y + 8) % 4) + (my_x - along_x + 8) % 4

    def seg_peer(t):
        return lax.rem(seg + t, n_seg)

    def seg_far_first(t):
        away = n_seg // 2 + (2 * (t % 2) - 1) * (t // 2)
        return lax.rem(seg + away, n_seg)

    def seg_source(t):
        return lax.rem(seg + n_seg - t, n_seg)

    def each(lo, hi, body):
        def step(t, carry):
            body(t)
            return carry

        lax.fori_loop(lo, hi, step, 0)

    def listed(d, e):
        return lax.rem(listed_at[e % RANDOM, 2 * d + e // RANDOM], n_blk)

    def arrived(ref, sem):
        pltpu.make_async_copy(ref, ref, sem).wait()

    def columns(j):
        return pl.ds(pl.multiple_of(j * DIM, DIM), DIM)

    barrier = pltpu.get_barrier_semaphore()

    def greet(t):
        pl.semaphore_signal(barrier, inc=1, device_id=(seg, peer(t)), device_id_type=MESH)

    def greet_seg(t):
        pl.semaphore_signal(barrier, inc=1, device_id=(seg_peer(t), me), device_id_type=MESH)

    each(1, n_dev, greet)
    each(1, n_seg, greet_seg)

    tok_g = pltpu.make_async_copy(grad_out, g_tok, tok_sem.at[0])
    tok_o = pltpu.make_async_copy(output, o_tok, tok_sem.at[1])
    tok_g.start()
    tok_o.start()

    inputs = (keys, values, query, grad_out)

    def landing(a, j):
        half = pl.ds((a % 2) * DIM, DIM)
        if a < 2:
            return kv.at[pl.ds(1 + 2 * j, 2), :, half]
        return qg.at[pl.ds(2 * j, 2), :, half]

    def head_in(a, j):
        return pltpu.make_async_remote_copy(
            src_ref=inputs[a].at[:, :, columns(j)],
            dst_ref=landing(a, me),
            send_sem=send_in.at[a // 2],
            recv_sem=recv_kv if a < 2 else recv_qg.at[me],
            device_id=(seg, j),
            device_id_type=MESH,
        )

    def own_in(a):
        return pltpu.make_async_copy(
            inputs[a].at[:, :, columns(me)], landing(a, me), local_in.at[a]
        )

    for a in range(4):
        own_in(a).start()

    pl.semaphore_wait(barrier, n_dev + n_seg - 2)

    def send_kv(t):
        head_in(0, peer(t)).start()
        head_in(1, peer(t)).start()

    def send_qg(t):
        head_in(2, peer(t)).start()
        head_in(3, peer(t)).start()

    each(1, n_dev, lambda t: send_kv(n_dev - t))

    tok_g.wait()
    tok_o.wait()
    lane = lax.broadcasted_iota(jnp.int32, (tok, HEADS), 1)
    delta = jnp.zeros((tok, HEADS), F32)
    for j in range(HEADS):
        part = pl.ds(j * DIM, DIM)
        product = g_tok[:, :, part].astype(F32) * o_tok[:, :, part].astype(F32)
        product = product.reshape(tok, DIM)
        delta = jnp.where(lane == j, jnp.sum(product, axis=1, keepdims=True), delta)
    lse_rows = lse_t[...].astype(F32)
    delta_t = jnp.transpose(delta.astype(BF16).astype(F32))
    for j in range(HEADS):
        stats_out[j, 0:1, :] = lse_rows[j : j + 1, :]
        stats_out[j, 1:2, :] = delta_t[j : j + 1, :]

    def stat(j):
        return pltpu.make_async_remote_copy(
            src_ref=stats_out.at[j],
            dst_ref=stats_in.at[me],
            send_sem=send_st,
            recv_sem=recv_st,
            device_id=(seg, j),
            device_id_type=MESH,
        )

    each(1, n_dev, lambda t: stat(peer(t)).start())
    stats_in[me] = stats_out[me]

    acc[...] = jnp.zeros_like(acc)
    prefix[0] = jnp.zeros_like(prefix[0])
    rim_zero = jnp.zeros((BLOCK, 2 * DIM), BF16)

    @pl.when(seg == 0)
    def _():
        kv[0] = rim_zero

    @pl.when(seg == n_seg - 1)
    def _():
        kv[n_blk + 1] = rim_zero

    block_lane = lax.broadcasted_iota(jnp.int32, (1, DIM), 1)

    def remember(t, latest):
        table[pl.ds(t, 1), :] = latest
        for k, e in enumerate(by_r):
            latest = jnp.where(block_lane == listed(source(t), e), t * refs + k + 1, latest)
        return latest

    latest = jnp.zeros((1, DIM), jnp.int32)
    table[pl.ds(n_pair, 1), :] = lax.fori_loop(0, n_pair, remember, latest)
    to_links = pltpu.make_async_copy(table, links, table_sem)
    to_links.start()

    each(1, QG_EARLY, send_qg)
    to_links.wait()

    own_in(0).wait()
    own_in(1).wait()

    arrived(kv.at[pl.ds(0, 2 * (n_dev - 1))], recv_kv)

    def rim_copy(side, src, dst, u, target):
        return pltpu.make_async_remote_copy(
            src_ref=src,
            dst_ref=dst,
            send_sem=send_rim.at[u, side],
            recv_sem=recv_rim.at[u, side],
            device_id=(target, me),
            device_id_type=MESH,
        )

    arrived(stats_in.at[pl.ds(0, n_dev - 1)], recv_st)
    kv_up = rim_copy(
        0, kv.at[n_blk], rim_kv.at[0], 0, seg_peer(1)
    )
    kv_down = rim_copy(
        1, kv.at[1], rim_kv.at[1], 0, seg_source(1)
    )
    grad_up = rim_copy(
        0, acc.at[pl.ds(BLOCK + seq_rows, BLOCK)], rim_in.at[0], 1, seg_peer(1)
    )
    grad_down = rim_copy(1, acc.at[pl.ds(0, BLOCK)], rim_in.at[1], 1, seg_source(1))
    has_next = seg < n_seg - 1
    has_prev = seg > 0

    @pl.when(has_next)
    def _():
        kv_up.start()

    @pl.when(has_prev)
    def _():
        kv_down.start()

    def scatter(u, c):
        return pltpu.make_async_remote_copy(
            src_ref=glob_x.at[u, rows(c, 8)],
            dst_ref=glob_rs.at[u, seg],
            send_sem=send_rs.at[u],
            recv_sem=recv_rs.at[u],
            device_id=(c, me),
            device_id_type=MESH,
        )

    def spread(u, c):
        return pltpu.make_async_remote_copy(
            src_ref=glob_red.at[u],
            dst_ref=glob_y.at[u, rows(seg, 8)],
            send_sem=send_ag.at[u],
            recv_sem=recv_ag.at[u],
            device_id=(c, me),
            device_id_type=MESH,
        )

    others = pl.ds(0, n_seg - 1)
    others_rows = pl.ds(0, 8 * (n_seg - 1))

    def sum_start(u):
        each(1, n_seg, lambda t: scatter(u, seg_far_first(t)).start())

    def sum_middle(u):
        arrived(glob_rs.at[u, others], recv_rs.at[u])
        total = glob_x[u, rows(seg, 8), :]
        for t in range(1, n_seg):
            total += glob_rs[u, seg_source(t)]
        glob_red[u] = total
        glob_y[u, rows(seg, 8), :] = total
        each(1, n_seg, lambda t: spread(u, seg_far_first(t)).start())

    def sum_end(u):
        arrived(glob_y.at[u, others_rows], recv_ag.at[u])

    def sum_drain(u):
        arrived(glob_rs.at[u, others], send_rs.at[u])
        arrived(glob_y.at[u, others_rows], send_ag.at[u])

    def key_block(at):
        return kv[at + 1]

    def owned(i):
        return jnp.where(glob_id[i] // n_blk == seg, 1.0, 0.0).astype(F32)

    for i in range(GLOBAL):
        glob_x[0, pl.ds(i * BLOCK, BLOCK), :] = (
            key_block(lax.rem(glob_id[i], n_blk)).astype(F32) * owned(i)
        )
    sum_start(0)
    each(QG_EARLY, QG_MIDDLE, send_qg)
    glob_x[1] = jnp.zeros((GLOBAL * BLOCK, 2 * DIM), F32)

    def out_copy(a, j):
        out, held = ((dq_hbm, dq_out), (dk_hbm, dk_out), (dv_hbm, dv_out))[a]
        return pltpu.make_async_remote_copy(
            src_ref=held.at[rows(j, tok)],
            dst_ref=out.at[:, columns(me)],
            send_sem=send_out.at[a],
            recv_sem=recv_out.at[a],
            device_id=(seg, j),
            device_id_type=MESH,
        )

    def own_out(a):
        out, held = ((dq_hbm, dq_out), (dk_hbm, dk_out), (dv_hbm, dv_out))[a]
        return pltpu.make_async_copy(
            held.at[rows(me, tok)], out.at[:, columns(me)], local_out.at[a]
        )

    lane = lax.broadcasted_iota(jnp.int32, (1, 2 * DIM), 1)
    scale = jnp.where(lane < DIM, 1.0, FACTOR).astype(F32)

    def pair(d):
        both = qg[pl.ds(2 * d, 2)].reshape(tok, 2 * DIM)
        q = both[:, :DIM]
        g = both[:, DIM:]
        lse = stats_in[d, 0:1, :]
        row_delta = stats_in[d, 1:2, :]
        zero = jnp.zeros((tok, DIM), BF16)
        into = jnp.concatenate(
            [jnp.concatenate([q, zero], 1), jnp.concatenate([zero, g], 1)], 0
        )
        back = jnp.concatenate(
            [jnp.concatenate([g, zero], 1), jnp.concatenate([zero, q], 1)], 0
        )

        def entries(block, active):
            both = lax.dot_general(
                block, into, (((1,), (1,)), ((), ())), preferred_element_type=F32
            )
            weights = jnp.exp(both[:, :DIM] * FACTOR - lse)
            if active is not None:
                weights = jnp.where(active, weights, 0.0)
            dscore = (weights * (both[:, DIM:] - row_delta)).astype(BF16)
            grads = jnp.dot(
                jnp.concatenate([weights.astype(BF16), dscore], 1),
                back,
                preferred_element_type=F32,
            )
            return grads * scale, dscore

        return entries

    def query_grad(dscore, block):
        return FACTOR * lax.dot_general(
            dscore, block[:, :DIM], (((0,), (0,)), ((), ())), preferred_element_type=F32
        )

    def places(count):
        key_at = lax.broadcasted_iota(jnp.int32, (count, tok), 0)
        query_at = lax.broadcasted_iota(jnp.int32, (count, tok), 1) // BLOCK
        return key_at // BLOCK, query_at

    def send_dq(t):
        d = source(t)

        @pl.when(t == 0)
        def _():
            own_out(0).start()

        @pl.when(t > 0)
        def _():
            out_copy(0, d).start()

    win, rand = 4 * BLOCK, 2 * BLOCK

    def wait_rows(t):
        d = source(t)

        @pl.when(t == 0)
        def _():
            own_in(2).wait()
            own_in(3).wait()

        @pl.when(t > 0)
        def _():
            arrived(qg.at[pl.ds(2 * d, 2)], recv_qg.at[d])

    def pair_part(t, late):
        d = source(t)

        @pl.when((d == 0) & has_prev)
        def _():
            kv_up.wait_recv()
            kv[0] = rim_kv[0]

        @pl.when((d == n_pair - 1) & has_next)
        def _():
            kv_down.wait_recv()
            kv[n_blk + 1] = rim_kv[1]

        key_at, query_at = places(win)
        absolute = seg * n_blk + 2 * d - 1 + key_at
        near = (
            (key_at >= query_at)
            & (key_at <= query_at + 2)
            & (absolute >= 0)
            & (absolute < n_seg * n_blk)
        )
        key_at, query_at = places(rand)
        own = key_at == query_at
        found = [listed(d, e) for e in by_r]
        block = jnp.concatenate(
            [kv[pl.ds(2 * d, 4)].reshape(win, 2 * DIM)] + [key_block(b) for b in found], 0
        )
        grads, dscore = pair(d)(block, jnp.concatenate([near] + [own] * RANDOM, 0))
        above = pl.ds(pl.multiple_of(d * tok, tok), BLOCK)
        inside = pl.ds(pl.multiple_of(d * tok + BLOCK, BLOCK), tok)
        below = pl.ds(pl.multiple_of(d * tok + BLOCK + tok, BLOCK), BLOCK)
        acc[above, :] += rounded(grads[:BLOCK])
        acc[inside, :] += grads[BLOCK : BLOCK + tok]
        acc[below, :] += rounded(grads[BLOCK + tok : win])
        dq = query_grad(dscore[:win], block[:win])
        if late:
            dq += dq_acc[rows(d, tok), :]
        for r in range(RANDOM):
            part = slice(win + r * rand, win + (r + 1) * rand)
            dq += rounded(query_grad(dscore[part], block[part]))
        if late:
            dq_out[rows(d, tok), :] = dq.astype(BF16)
        else:
            dq_acc[rows(d, tok), :] = dq
        for k, b in enumerate(found):
            at = win + k * BLOCK
            prefix[t * refs + k + 1] = rounded(grads[at : at + BLOCK]) + prefix[links[t, b]]

    def global_part(t, late):
        d = source(t)
        block = glob_kv[...]
        grads, dscore = pair(d)(block, None)
        glob_x[1] += grads
        dq = query_grad(dscore, block)
        if late:
            dq_acc[rows(d, tok), :] = dq
        else:
            dq_out[rows(d, tok), :] = (dq + dq_acc[rows(d, tok), :]).astype(BF16)

    half = n_pair // 2

    def early(t):
        wait_rows(t)
        pair_part(t, False)

    def globals_of(t):
        global_part(t - half, False)
        wait_rows(t)
        global_part(t, True)

    def late(t):
        pair_part(t, True)
        send_dq(t)

    each(0, 2, early)
    sum_middle(0)
    each(QG_MIDDLE, n_dev, send_qg)
    each(2, half, early)
    sum_end(0)
    glob_kv[...] = glob_y[0].astype(BF16)
    each(half, n_pair, globals_of)

    sum_start(1)
    each(0, half, send_dq)
    each(half, LATE, late)
    sum_middle(1)
    each(LATE, n_pair, late)

    @pl.when(has_next)
    def _():
        grad_up.start()

    @pl.when(has_prev)
    def _():
        grad_down.start()

    @pl.when(has_prev)
    def _():
        grad_up.wait_recv()
        acc[pl.ds(BLOCK, BLOCK), :] += rim_in[0]

    @pl.when(has_next)
    def _():
        grad_down.wait_recv()
        acc[pl.ds(seq_rows, BLOCK), :] += rim_in[1]

    sum_end(1)

    def finish(t):
        d = source(t)
        for i in range(2):
            b = 2 * d + i
            at = pl.ds(pl.multiple_of(b * BLOCK, BLOCK), BLOCK)
            total = acc[pl.ds(pl.multiple_of(BLOCK + b * BLOCK, BLOCK), BLOCK), :]
            total += prefix[links[n_pair, b]]
            for j in range(GLOBAL):
                here = jnp.where(glob_id[j] == seg * n_blk + b, 1.0, 0.0).astype(F32)
                total += glob_y[1, pl.ds(j * BLOCK, BLOCK), :] * here
            dv_out[at, :] = total[:, :DIM].astype(BF16)
            dk_out[at, :] = total[:, DIM:].astype(BF16)

        @pl.when(t == 0)
        def _():
            own_out(1).start()
            own_out(2).start()

        @pl.when(t > 0)
        def _():
            out_copy(1, d).start()
            out_copy(2, d).start()

    each(0, n_pair, lambda t: finish(n_pair - 1 - t))

    sum_drain(0)
    sum_drain(1)

    @pl.when(has_next)
    def _():
        kv_up.wait_send()
        grad_up.wait_send()

    @pl.when(has_prev)
    def _():
        kv_down.wait_send()
        grad_down.wait_send()

    most = pl.ds(0, 2 * (n_dev - 1))
    arrived(kv.at[most], send_in.at[0])
    arrived(qg.at[most], send_in.at[1])
    arrived(stats_out.at[pl.ds(0, n_dev - 1)], send_st)
    for a, (out, held) in enumerate(((dq_hbm, dq_out), (dk_hbm, dk_out), (dv_hbm, dv_out))):
        arrived(held.at[pl.ds(0, (n_dev - 1) * tok)], send_out.at[a])
        own_out(a).wait()
        arrived(out.at[:, pl.ds(0, (n_dev - 1) * DIM)], recv_out.at[a])


def shards(query, keys, values, output, grad_out, log_sum_exp, random_blocks, global_blocks):
    tok, width = query.shape
    query, keys, values, output, grad_out = (
        x.reshape(2, BLOCK, width) for x in (query, keys, values, output, grad_out)
    )
    n_seg, n_dev = lax.axis_size("pb"), lax.axis_size("ka")
    refs = 2 * RANDOM
    n_blk = 2 * n_dev
    count = n_dev * refs

    smem = pl.BlockSpec(memory_space=pltpu.SMEM)
    hbm = pl.BlockSpec(memory_space=pltpu.HBM)
    vmem = pl.BlockSpec(memory_space=pltpu.VMEM)
    dma = pltpu.SemaphoreType.DMA
    seq = n_dev * tok
    glob = GLOBAL * BLOCK
    out = jax.ShapeDtypeStruct((tok, width), BF16)
    grads = pl.pallas_call(
        functools.partial(kernel, n_seg, n_dev),
        out_shape=(out, out, out),
        in_specs=[smem, smem, hbm, hbm, hbm, hbm, hbm, vmem],
        out_specs=(hbm, hbm, hbm),
        scratch_shapes=[
            pltpu.VMEM((n_blk + 2, BLOCK, 2 * DIM), BF16),
            pltpu.VMEM((n_blk, BLOCK, 2 * DIM), BF16),
            pltpu.VMEM((seq + 2 * BLOCK, 2 * DIM), F32),
            pltpu.VMEM((count + 1, BLOCK, 2 * DIM), F32),
            pltpu.VMEM((seq, DIM), F32),
            pltpu.VMEM((seq, DIM), BF16),
            pltpu.VMEM((seq, DIM), BF16),
            pltpu.VMEM((seq, DIM), BF16),
            pltpu.VMEM((2, BLOCK, width), BF16),
            pltpu.VMEM((2, BLOCK, width), BF16),
            pltpu.VMEM((n_dev, 8, tok), F32),
            pltpu.VMEM((n_dev, 8, tok), F32),
            pltpu.VMEM((2, glob, 2 * DIM), F32),
            pltpu.VMEM((2, n_seg, 8, 2 * DIM), F32),
            pltpu.VMEM((2, 8, 2 * DIM), F32),
            pltpu.VMEM((2, glob, 2 * DIM), F32),
            pltpu.VMEM((glob, 2 * DIM), BF16),
            pltpu.VMEM((2, BLOCK, 2 * DIM), BF16),
            pltpu.VMEM((2, BLOCK, 2 * DIM), F32),
            pltpu.VMEM((n_dev + 8, DIM), jnp.int32),
            pltpu.SMEM((n_dev + 8, DIM), jnp.int32),
            dma((2,)),
            dma(()),
            dma((n_dev,)),
            dma((4,)),
            dma(()),
            dma(()),
            dma((3,)),
            dma((3,)),
            dma((3,)),
            dma((2,)),
            dma((2,)),
            dma((2,)),
            dma((2,)),
            dma((2, 2)),
            dma((2, 2)),
            dma((2,)),
            dma(()),
        ],
        compiler_params=pltpu.CompilerParams(
            collective_id=0, has_side_effects=True, vmem_limit_bytes=52 * 2**20
        ),
        cost_estimate=pl.CostEstimate(
            flops=2**32, bytes_accessed=2**23, transcendentals=2**21
        ),
    )(jnp.transpose(random_blocks), global_blocks, query, keys, values, output, grad_out, jnp.transpose(log_sum_exp))
    return grads


def solution(mesh):
    both = P(("pb", "ka"), None)
    return jax.shard_map(
        shards,
        mesh=mesh,
        in_specs=(both, both, both, both, both, both, P("pb", None), P()),
        out_specs=(both, both, both),
        check_vma=False,
    )
```
